256 devices in a mesh: lat: 32 (over x, z_lo, core), lon: 8 (over z_hi, y).
Axes of the slice: x: 4, y: 4, z: 8 (z_hi: 2, z_lo: 4; z = z_hi * 4 + z_lo), core: 2. Of those that a mesh axis runs over, the one named last changes fastest.
Arguments:
- grid_input: bfloat16 [704, 1440, 256], P('lat', 'lon'), may hold values from -1.5 to 1.5
- cotangent: bfloat16 [704, 1440, 256], P('lat', 'lon'), may hold values from -6 to 6
- mixing: bfloat16 [384, 256, 256], P('lat', 'lon'), may hold values from -0.375 to 0.375
Outputs:
- input_grad: bfloat16 [704, 1440, 256], P('lat', 'lon')
- weight_grad: float32 [384, 256, 256], P('lat', 'lon')
The draws below stay inside these ranges and needn't reach their ends.
All inputs are finite; a program needn't handle non-finite values.
Results may differ from the reference program's by a relative error of at most 0.0083.
Values may be sent and summed in bfloat16 or wider, within the bound.
No kernel may reach another device: no remote copies, remote signals or barrier semaphores. Data moves between devices by JAX's collectives and lax.ppermute only.
A program may use at most 128 MiB of HBM per device.

```python
import math
import jax
import jax.numpy as jnp
from jax import lax

C = 256
NLON = 1440
LAT_DEV = 22
ORD_DEV = 12
NLAT = 704
M = 384
L = 384
N_LAT = 32


def shard_levels(key, extent, shards, low, top_value):
    level = 1.0
    for position, shards_of in shards:
        heights = jax.random.uniform(jax.random.fold_in(jax.random.fold_in(key, 6), position), (shards_of,), jnp.float32, low / len(shards), top_value / len(shards))
        level = level * jnp.repeat(jnp.exp(heights), extent[position] // shards_of).reshape((-1,) + (1,) * (len(extent) - 1 - position))
    return level


def noise(stream_key, dims, spread, reach, cuts=(), kind=jnp.bfloat16):
    values = jax.random.normal(stream_key, dims, jnp.float32) * spread
    if len(cuts) > 0:
        values = shard_levels(stream_key, dims, cuts, -0.22, 0.18) * values
    return jnp.clip(values, min=-reach, max=reach).astype(kind)


def setup_inputs(seed: int = 0) -> dict:
    splits = jax.random.split(jax.random.key(seed), 4)
    return {
        "grid_input": noise(splits[0], (NLAT, NLON, C), 0.25, 1.5, ((0, 32), (1, 8))),
        "cotangent": noise(splits[1], (NLAT, NLON, C), 1.0, 6.0, ((0, 32), (1, 8))),
        "mixing": noise(splits[2], (L, C, C), C ** -0.5, 0.375, ((0, 32), (1, 8))),
    }


def quadrature(count_lat):
    colatitude = (jnp.arange(count_lat, dtype=jnp.float32) + 0.5) * (math.pi / count_lat)
    return math.pi / count_lat * jnp.sin(colatitude)

def degree_block(degrees):
    for width in (16, 8, 4, 2):
        if degrees % width == 0:
            return width
    return 1

def legendre_table(order_ids, count_lat, degrees, order_cap):
    colatitude = (jnp.arange(count_lat, dtype=jnp.float32) + 0.5) * (math.pi / count_lat)
    cosine = jnp.cos(colatitude)[None, :]
    sine_row = jnp.sin(colatitude)[None, :]
    order_value = order_ids.astype(jnp.float32)[:, None]
    counter = jnp.arange(1, order_cap + 1, dtype=jnp.float32)[None, :]
    log_terms = jnp.where(counter <= order_value, jnp.log1p(0.5 / counter), 0.0)
    log_start = 0.5 * math.log(0.5) + 0.5 * lax.optimization_barrier(jnp.sum(log_terms, axis=1, keepdims=True)) + order_value * jnp.log(sine_row)
    zero_state = jnp.zeros((order_ids.shape[0], count_lat), jnp.float32)
    width = degree_block(degrees)

    def advance(carried, degree):
        previous, earlier, scale_log = carried
        growth = jnp.sqrt((4.0 * degree * degree - 1.0) / jnp.maximum(degree * degree - order_value * order_value, 1.0))
        shrink = jnp.sqrt(jnp.maximum((degree - 1.0) * (degree - 1.0) - order_value * order_value, 0.0) / jnp.maximum(4.0 * (degree - 1.0) * (degree - 1.0) - 1.0, 1.0))
        recurred = growth * (cosine * previous - shrink * earlier)
        first_step = cosine * jnp.sqrt(2.0 * order_value + 3.0) * previous
        current = jnp.where(degree == order_value, 1.0, jnp.where(degree == order_value + 1.0, first_step, jnp.where(degree > order_value, recurred, 0.0)))
        oversized = jnp.abs(current) > 10000000000.0
        factor = jnp.where(oversized, 1e-10, 1.0)
        scale_log = scale_log + jnp.where(oversized, math.log(10000000000.0), 0.0)
        current = current * factor
        stored = (current * jnp.exp(scale_log)).astype(jnp.bfloat16)
        return ((current, previous * factor, scale_log), stored)

    def advance_block(carried, block_start):
        stored_list = []
        for step in range(width):
            carried, stored = advance(carried, block_start + float(step))
            stored_list.append(stored)
        return (carried, jnp.stack(stored_list, axis=0))
    initial = (zero_state, zero_state, log_start + zero_state)
    starts = jnp.arange(degrees // width, dtype=jnp.float32) * float(width)
    _, blocks = lax.scan(advance_block, initial, starts)
    return blocks.reshape(degrees, order_ids.shape[0], count_lat)

def fourier_tables(order_ids, count_lon):
    points = jnp.arange(count_lon, dtype=jnp.int32)
    phase_index = points[:, None] * order_ids[None, :] % count_lon
    angles = phase_index.astype(jnp.float32) * (2.0 * math.pi / count_lon)
    forward = jnp.stack([jnp.cos(angles), -jnp.sin(angles)], axis=2).reshape(count_lon, 2 * order_ids.shape[0])
    factor = jnp.where(order_ids == 0, 1.0, 2.0).astype(jnp.float32) / count_lon
    backward = forward * jnp.repeat(factor, 2)[None, :]
    return (forward.astype(jnp.bfloat16), backward.astype(jnp.bfloat16))

def reference(grid_input, cotangent, mixing):
    order_ids = jnp.arange(M, dtype=jnp.int32)
    forward, backward = fourier_tables(order_ids, NLON)
    forward_f = forward.astype(jnp.float32)
    backward_f = backward.astype(jnp.float32)
    weights = quadrature(NLAT)

    def analyse_rows(row_block):
        block_x, block_g, block_w = row_block
        spec_x = jnp.einsum('jkc,kq->jqc', block_x.astype(jnp.float32), forward_f) * block_w[:, None, None]
        spec_g = jnp.einsum('jkc,kq->jqc', block_g.astype(jnp.float32), backward_f)
        return (spec_x.astype(jnp.bfloat16), spec_g.astype(jnp.bfloat16))
    spectra_x, spectra_g = lax.map(analyse_rows, (grid_input.reshape(N_LAT, LAT_DEV, NLON, C), cotangent.reshape(N_LAT, LAT_DEV, NLON, C), weights.reshape(N_LAT, LAT_DEV)))
    spectra_x = spectra_x.reshape(NLAT, 2 * M, C)
    spectra_g = spectra_g.reshape(NLAT, 2 * M, C)
    mixing_f = mixing.astype(jnp.float32)

    def per_block(grad_total, block_index):
        first_order = block_index * ORD_DEV
        legendre = legendre_table(first_order + jnp.arange(ORD_DEV, dtype=jnp.int32), NLAT, L, M).astype(jnp.float32)
        piece_x = lax.dynamic_slice_in_dim(spectra_x, 2 * first_order, 2 * ORD_DEV, 1).astype(jnp.float32).reshape(NLAT, ORD_DEV, 2, C)
        piece_g = lax.dynamic_slice_in_dim(spectra_g, 2 * first_order, 2 * ORD_DEV, 1).astype(jnp.float32).reshape(NLAT, ORD_DEV, 2, C)
        coefficients = lax.optimization_barrier(jnp.einsum('lmj,jmrc->mlrc', legendre, piece_x).astype(jnp.bfloat16)).astype(jnp.float32)
        adjoint = lax.optimization_barrier(jnp.einsum('lmj,jmrc->mlrc', legendre, piece_g).astype(jnp.bfloat16)).astype(jnp.float32)
        mixed = lax.optimization_barrier(jnp.einsum('mlrc,lic->mlri', adjoint, mixing_f).astype(jnp.bfloat16)).astype(jnp.float32)
        grad_total = grad_total + jnp.einsum('mlri,mlrc->lic', coefficients, adjoint)
        back_rows = jnp.einsum('lmj,mlrc->jmrc', legendre, mixed) * weights[:, None, None, None]
        return (grad_total, back_rows.astype(jnp.bfloat16).reshape(NLAT, 2 * ORD_DEV, C))
    weight_grad, pieces = lax.scan(per_block, jnp.zeros((L, C, C), jnp.float32), jnp.arange(N_LAT, dtype=jnp.int32))
    spectral_back = jnp.transpose(pieces, (1, 0, 2, 3)).reshape(NLAT, 2 * M, C)

    def synthesise_rows(row_block):
        block_h, block_g = row_block
        grid_back = jnp.einsum('jqc,kq->jkc', block_h.astype(jnp.float32), forward_f)
        grid_back = lax.optimization_barrier(grid_back.astype(jnp.bfloat16)).astype(jnp.float32)
        return (block_g.astype(jnp.float32) + grid_back).astype(jnp.bfloat16)
    input_grad = lax.map(synthesise_rows, (spectral_back.reshape(N_LAT, LAT_DEV, 2 * M, C), cotangent.reshape(N_LAT, LAT_DEV, NLON, C)))
    return (input_grad.reshape(NLAT, NLON, C), weight_grad)
```

```python
import math

import jax
import jax.numpy as jnp
from jax import lax
from jax.experimental import pallas as pl
from jax.experimental.pallas import tpu as pltpu
from jax.sharding import Mesh, PartitionSpec as P

F32 = jnp.float32
BF16 = jnp.bfloat16
NLON, NLAT, ORDERS, DEGREES = 1440, 704, 384, 384
ROWS, POINTS, CH = 22, 180, 256
RING = ("zlo", "zhi", "y")
CROSS = ("x", "core")
NT = (((1,), (1,)), ((), ()))
TN = (((0,), (0,)), ((), ()))
SMEM = pl.BlockSpec(memory_space=pltpu.SMEM)
PIECE = jax.ShapeDtypeStruct((768, 128), BF16)


def call(body, outs, ins, grid=(1,), scratch=(), us=1, specs=None, out_specs=None, name=None):
    whole = lambda a: pl.BlockSpec(a.shape, lambda *_, n=len(a.shape): (0,) * n)
    specs = specs or [None] * len(ins)
    return pl.pallas_call(
        body,
        out_shape=outs,
        grid=grid,
        in_specs=[whole(a) if s is None else s for a, s in zip(ins, specs)],
        out_specs=out_specs or jax.tree.map(whole, outs),
        scratch_shapes=list(scratch),
        compiler_params=pltpu.CompilerParams(vmem_limit_bytes=56 * 2**20),
        cost_estimate=pl.CostEstimate(
            flops=us * 1_100_000_000, bytes_accessed=us * 1_000_000, transcendentals=0
        ),
        name=name,
    )(*ins)


def partner(position, k):
    dx, dc = divmod(k, 2)
    x, core = position // 2, position % 2
    core = (core + dc) % 2
    return ((x + dx) % 4) * 2 + core, ((x + 4 - dx) % 4) * 2 + core


def pack_kernel(p_ref, x_ref, o_ref, s_ref):
    south = p_ref[0] >= 4
    eye = (
        lax.broadcasted_iota(jnp.int32, (CH, CH), 0) == lax.broadcasted_iota(jnp.int32, (CH, CH), 1)
    ).astype(BF16)
    zeros = jnp.zeros((CH, 76), F32)
    for pair in range(11):
        tail = None
        for parity in range(2):
            j = 2 * pair + parity
            j = jnp.where(south, 21 - j, j)
            head = lax.dot_general(eye, x_ref[j, 0:128, :], NT, preferred_element_type=F32)
            row = (parity * 11 + pair) * 8
            s_ref[:, row : row + 8, :] = head.reshape(32, 8, 128)
            rest = lax.dot_general(eye, x_ref[j, 128:180, :], NT, preferred_element_type=F32)
            rest = jnp.concatenate([rest, zeros], axis=1)
            tail = rest if parity == 0 else tail + pltpu.roll(rest, 64, 1)
        row = 176 + pair * 8
        s_ref[:, row : row + 8, :] = tail.reshape(32, 8, 128)
    o_ref[...] = s_ref[...].astype(BF16)


def pack(position, x):
    return call(
        pack_kernel,
        jax.ShapeDtypeStruct((32, 264, 128), BF16),
        [position, x],
        scratch=[pltpu.VMEM((32, 264, 128), F32)],
        specs=[SMEM, None],
        us=5,
        name="pack",
    )


def waves_kernel(c_ref, s_ref, f_ref, b_ref):
    for d in range(8):
        rows = slice(d * 96, d * 96 + 96)
        order = 8 * (lax.broadcasted_iota(jnp.int32, (96, 128), 0) // 2) + d
        factor = jnp.where(order == 0, 1.0 / NLON, 2.0 / NLON)
        low = lax.broadcasted_iota(jnp.int32, (96, 128), 1) < 64

        def turned(o, lanes):
            angle = (d * o) % 8 * math.pi / 4
            return c_ref[rows, lanes] * math.cos(angle) - s_ref[rows, lanes] * math.sin(angle)

        def put(value, place):
            f_ref[rows, place * 128 : place * 128 + 128] = value.astype(BF16)
            b_ref[rows, place * 128 : place * 128 + 128] = (value * factor).astype(BF16)

        for o in range(8):
            put(turned(o, slice(0, 128)), o)
        for o in range(4):
            tails = [turned(2 * o + i, slice(128, 256)) for i in range(2)]
            put(jnp.where(low, tails[0], tails[1]), 8 + o)


def fourier_tables():
    q = jnp.arange(768, dtype=jnp.int32)
    order, quarter = 8 * (q % 96 // 2) + q // 96, q % 2
    lane = jnp.arange(256, dtype=jnp.int32)
    point = jnp.where(lane < 128, lane, 128 + lane % 64)
    valid = (point < POINTS)[None, :]
    phase = (point[None, :] * order[:, None] + 360 * quarter[:, None]) % NLON
    angle = phase.astype(F32) * (2.0 * math.pi / NLON)
    table = jax.ShapeDtypeStruct((768, 1536), BF16)
    return call(
        waves_kernel,
        (table, table),
        [jnp.where(valid, jnp.cos(angle), 0.0), jnp.where(valid, jnp.sin(angle), 0.0)],
        us=4,
        name="waves",
    )


def fourier_kernel(p_ref, r_ref, f_ref, w_ref, *refs):
    o_refs, (s_ref, k_ref, t_ref) = refs[:8], refs[8:]
    position = p_ref[0]
    south = position >= 4
    s_ref[0 : 32 * 264, :] = r_ref[...].reshape(32 * 264, 128).astype(F32)
    s_ref[32 * 264 :, :] = jnp.zeros((64, 128), F32)
    low = lax.broadcasted_iota(jnp.int32, (16, 128), 1) < 64

    def one(pair, _):
        for b in range(2):
            c = 2 * pair + b
            for zlo in range(4):
                source = jnp.where(south, 3 - zlo, zlo) * (8 * 264) + c
                row = b * 128 + zlo * 32
                tails = []
                for o in range(8):
                    base = source + o * 264
                    for parity in range(2):
                        k_ref[row + parity * 16 : row + parity * 16 + 16, o * 128 : o * 128 + 128] = (
                            s_ref[pl.ds(base + parity * 88, 16, stride=8), :].astype(BF16)
                        )
                    tails.append(s_ref[pl.ds(base + 176, 16, stride=8), :])
                for o in range(4):
                    even, odd = tails[2 * o], tails[2 * o + 1]
                    lanes = slice(1024 + o * 128, 1152 + o * 128)
                    north = jnp.where(low, even, pltpu.roll(odd, 64, 1))
                    k_ref[row : row + 16, lanes] = north.astype(BF16)
                    other = jnp.where(low, pltpu.roll(even, 64, 1), odd)
                    k_ref[row + 16 : row + 32, lanes] = other.astype(BF16)
        spec = lax.dot_general(f_ref[...], k_ref[...], NT, preferred_element_type=F32)
        for b in range(2):
            value = spec[:, b * 128 : b * 128 + 128] * w_ref[0:1, :]
            t_ref[pl.ds(2 * pair + b, 768, stride=8), :] = value
        return 0

    lax.fori_loop(0, 4, one, 0)
    for k in range(8):
        start = pl.multiple_of(partner(position, k)[0] * 768, 768)
        o_refs[k][...] = t_ref[pl.ds(start, 768), :].astype(BF16)


def fourier(position, received, table, weights):
    return call(
        fourier_kernel,
        (PIECE,) * 8,
        [position, received, table, weights],
        scratch=[
            pltpu.VMEM((32 * 264 + 64, 128), F32),
            pltpu.VMEM((256, 1536), BF16),
            pltpu.VMEM((6144, 128), F32),
        ],
        specs=[SMEM, None, None, None],
        us=9,
        name="fourier",
    )


def block_orders(i):
    return jnp.where(i < 6, i // 3, jnp.where(i < 10, 2 + (i - 6) // 2, i - 6))


def block_degrees(i):
    return jnp.where(i < 6, i % 3, jnp.where(i < 10, 1 + i % 2, 2))


def table_kernel(m_ref, cos_ref, log_ref, o_ref, s_ref, v_ref):
    i = pl.program_id(0)
    group, part = block_orders(i), block_degrees(i)

    @pl.when(part == group // 2)
    def _():
        v_ref[0] = jnp.zeros((8, 512), F32)
        v_ref[1] = jnp.zeros((8, 512), F32)
        v_ref[2] = log_ref[...]

    order = m_ref[...]
    square = order * order
    cosine = cos_ref[...]
    wide = lambda a: jnp.concatenate([a] * 4, axis=1)

    def steps(n, carried):
        previous, earlier, scale = carried
        size = jnp.exp(scale)
        for u in range(8):
            l = n * 8 + u
            degree = jnp.full((8, 128), part * 128 + l, jnp.int32).astype(F32)
            below = (degree - 1.0) * (degree - 1.0)
            growth = jnp.sqrt(
                jnp.maximum(4.0 * degree * degree - 1.0, 0.0)
                / jnp.maximum(degree * degree - square, 1.0)
            )
            shrink = jnp.sqrt(
                jnp.maximum(below - square, 0.0) / jnp.maximum(4.0 * below - 1.0, 1.0)
            )
            current = wide(growth) * (cosine * previous) - wide(growth * shrink) * earlier
            current = jnp.where(wide(degree == order), 1.0, current)
            value = current * size
            for d in range(4):
                s_ref[d, pl.ds(pl.multiple_of(l * 8, 8), 8), :] = value[:, d * 128 : d * 128 + 128]
            previous, earlier = current, previous
        over = jnp.maximum(jnp.abs(previous), jnp.abs(earlier)) > 1e5
        factor = jnp.where(over, 1e-10, 1.0)
        scale = scale + jnp.where(over, math.log(1e10), 0.0)
        return previous * factor, earlier * factor, scale

    state = lax.fori_loop(0, 16, steps, (v_ref[0], v_ref[1], v_ref[2]))
    for n in range(3):
        v_ref[n] = state[n]
    for s in range(8):
        for d in range(4):
            o_ref[0, s, :, d * 128 : d * 128 + 128] = s_ref[
                d, pl.ds(s, 128, stride=8), :
            ].astype(BF16)


def legendre_table(orders, cosine, logs):
    return call(
        table_kernel,
        jax.ShapeDtypeStruct((12, 8, 128, 512), BF16),
        [orders, cosine, logs],
        grid=(12,),
        scratch=[pltpu.VMEM((4, 1024, 128), F32), pltpu.VMEM((3, 8, 512), F32)],
        specs=[
            pl.BlockSpec((8, 128), lambda i: (block_orders(i), 0)),
            None,
            pl.BlockSpec((8, 512), lambda i: (block_orders(i), 0)),
        ],
        out_specs=pl.BlockSpec((1, 8, 128, 512), lambda i: (i, 0, 0, 0)),
        us=25,
        name="legendre",
    )


def pick(g, *values):
    out = values[-1]
    for n in reversed(range(len(values) - 1)):
        out = jnp.where(g == n, values[n], out)
    return out


TABLE = [
    pl.BlockSpec((1, 8, 128, 512), lambda g, v=v: (pick(g, *v), 0, 0, 0))
    for v in ((0, 3), (1, 4, 6, 8), (2, 5, 7, 9, 10, 11))
]


def by_parts(group, body):
    for first in range(3):

        @pl.when(group // 2 == first)
        def _(first=first):
            body(first)


def signs(position, rows):
    lane = lax.broadcasted_iota(jnp.int32, (rows, 128), 1)
    return jnp.where((lane + position) % 2 == 0, 1.0, -1.0)


def analyse_kernel(p_ref, *refs):
    pieces, t_refs, (o_ref, s_ref, c_ref, q_ref) = refs[:8], refs[8:11], refs[11:]
    group = pl.program_id(0)
    position = p_ref[0]

    @pl.when(group == 0)
    def _():
        for k in range(8):
            s_ref[partner(position, k)[1]] = pieces[k][...]
        c_ref[...] = jnp.zeros_like(c_ref)

    sign = signs(position, 16)

    def body(first):
        for s in range(8):
            row = pl.multiple_of(group * 128 + s * 16, 16)
            north = jnp.concatenate([s_ref[d, pl.ds(row, 16), :] for d in range(4)], axis=1)
            south = jnp.concatenate([s_ref[7 - d, pl.ds(row, 16), :] for d in range(4)], axis=1)
            value = lax.dot_general(
                jnp.concatenate([north, south], axis=0),
                jnp.concatenate([t_refs[b][0, s] for b in range(first, 3)], axis=0),
                NT,
                preferred_element_type=F32,
            )
            for b in range(first, 3):
                lanes = slice((b - first) * 128, (b - first) * 128 + 128)
                c_ref[b, pl.ds(row, 16), :] = value[0:16, lanes] + sign * value[16:32, lanes]

    by_parts(group, body)

    @pl.when(group == 5)
    def _():
        lane = lax.broadcasted_iota(jnp.int32, (96, 128), 1)
        for c in range(8):
            block = jnp.concatenate(
                [c_ref[b, pl.ds(c, 96, stride=8), :] for b in range(3)], axis=1
            )
            block = jnp.concatenate([block, jnp.zeros((32, DEGREES), F32)], axis=0).T
            first = jnp.where(lane < 96, block[288:384], pltpu.roll(block[0:96], 96, 1))
            second = jnp.where(lane < 72, block[192:288], pltpu.roll(block[96:192], 72, 1))
            q_ref[0, pl.ds(c, 96, stride=8), :] = first
            q_ref[1, pl.ds(c, 96, stride=8), :] = second
        o_ref[...] = jnp.concatenate(
            [q_ref[0].reshape(32, 24, 128), q_ref[1].reshape(32, 24, 128)], axis=1
        ).astype(BF16)


def analyse(position, pieces, table):
    return call(
        analyse_kernel,
        jax.ShapeDtypeStruct((32, 48, 128), BF16),
        [position, *pieces, table, table, table],
        grid=(6,),
        scratch=[
            pltpu.VMEM((8, 768, 128), BF16),
            pltpu.VMEM((3, 768, 128), F32),
            pltpu.VMEM((2, 768, 128), F32),
        ],
        specs=[SMEM] + [None] * 8 + TABLE,
        us=10,
        name="analyse",
    )


def pair_rows(ref, p):
    return ref[:, p * 8 : p * 8 + 8, :].astype(F32).reshape(CH, 128).astype(BF16)


def mix_kernel(a_ref, w_ref, o_ref):
    lane = lax.broadcasted_iota(jnp.int32, (CH, 128), 1)
    pieces = []
    for p in range(6):
        half, e = divmod(p, 3)
        rows = pair_rows(a_ref, p)
        high = jnp.dot(w_ref[3 - half, :, e].reshape(CH, CH), rows, preferred_element_type=F32)
        low = jnp.dot(w_ref[half, :, e].reshape(CH, CH), rows, preferred_element_type=F32)
        pieces.append(jnp.where(lane < 96 - 24 * half, high, low).reshape(32, 8, 128))
    o_ref[...] = jnp.concatenate(pieces, axis=1).astype(BF16)


def mix(adjoint, mixing):
    return call(
        mix_kernel,
        jax.ShapeDtypeStruct((32, 48, 128), BF16),
        [adjoint, mixing],
        us=3,
        name="mix",
    )


def grad_kernel(c_ref, a_ref, o_ref):
    lane = lax.broadcasted_iota(jnp.int32, (CH, 128), 1)
    for p in range(6):
        half, e = divmod(p, 3)
        left, right = pair_rows(c_ref, p), pair_rows(a_ref, p)
        inside = lane < 96 - 24 * half
        zero = jnp.zeros_like(left)
        high = lax.dot_general(jnp.where(inside, left, zero), right, NT, preferred_element_type=F32)
        low = lax.dot_general(jnp.where(inside, zero, left), right, NT, preferred_element_type=F32)
        o_ref[3 - half, :, e] = high.reshape(2, 128, CH)
        o_ref[half, :, e] = low.reshape(2, 128, CH)


def weight_sums(coefficients, adjoint):
    return call(
        grad_kernel,
        jax.ShapeDtypeStruct((4, 2, 3, 128, CH), F32),
        [coefficients, adjoint],
        us=3,
        name="grad",
    )


def synthesise_kernel(p_ref, m_ref, w_ref, *refs):
    t_refs, o_refs, (q_ref, c_ref, b_ref) = refs[:3], refs[3:11], refs[11:]
    group = pl.program_id(0)
    position = p_ref[0]

    @pl.when(group == 0)
    def _():
        mixed = m_ref[...].astype(F32)
        q_ref[0] = mixed[:, 0:24, :].reshape(768, 128)
        q_ref[1] = mixed[:, 24:48, :].reshape(768, 128)
        for c in range(8):
            first = q_ref[0, pl.ds(c, 96, stride=8), :]
            second = q_ref[1, pl.ds(c, 96, stride=8), :]
            block = jnp.concatenate(
                [pltpu.roll(first, 32, 1), pltpu.roll(second, 56, 1), second, first], axis=0
            )
            block = block.T[0:96, :]
            for b in range(3):
                c_ref[b, pl.ds(c, 96, stride=8), :] = block[:, b * 128 : b * 128 + 128]

    sign = signs(position, 16)

    def body(first):
        for s in range(8):
            row = pl.multiple_of(group * 128 + s * 16, 16)
            north = [c_ref[b, pl.ds(row, 16), :] for b in range(first, 3)]
            south = [a * sign for a in north]
            left = jnp.concatenate(
                [jnp.concatenate(north, axis=1), jnp.concatenate(south, axis=1)], axis=0
            ).astype(BF16)
            right = jnp.concatenate([t_refs[b][0, s] for b in range(first, 3)], axis=0)
            value = jnp.dot(left, right, preferred_element_type=F32)
            for d in range(4):
                lanes = slice(d * 128, d * 128 + 128)
                mirror = slice((7 - d) * 128, (7 - d) * 128 + 128)
                b_ref[d, pl.ds(row, 16), :] = (value[0:16, lanes] * w_ref[0:1, lanes]).astype(BF16)
                b_ref[7 - d, pl.ds(row, 16), :] = (
                    value[16:32, lanes] * w_ref[0:1, mirror]
                ).astype(BF16)

    by_parts(group, body)

    @pl.when(group == 5)
    def _():
        for k in range(8):
            o_refs[k][...] = b_ref[partner(position, k)[0]]


def synthesise(position, mixed, table, weights):
    return call(
        synthesise_kernel,
        (PIECE,) * 8,
        [position, mixed, weights, table, table, table],
        grid=(6,),
        scratch=[
            pltpu.VMEM((2, 768, 128), F32),
            pltpu.VMEM((3, 768, 128), F32),
            pltpu.VMEM((8, 768, 128), BF16),
        ],
        specs=[SMEM, None, None] + TABLE,
        us=10,
        name="synthesise",
    )


def inverse_kernel(p_ref, *refs):
    pieces, (f_ref, o_ref, s_ref, t_ref) = refs[:8], refs[8:]
    position = p_ref[0]
    south = position >= 4
    for k in range(8):
        start = pl.multiple_of(partner(position, k)[1] * 768, 768)
        s_ref[pl.ds(start, 768), :] = pieces[k][...].astype(F32)
    low = lax.broadcasted_iota(jnp.int32, (11, 128), 1) < 64

    def one(pair, _):
        left = jnp.concatenate(
            [s_ref[pl.ds(2 * pair + b, 768, stride=8), :].astype(BF16) for b in range(2)], axis=1
        )
        grid = lax.dot_general(left, f_ref[...], TN, preferred_element_type=F32)
        for b in range(2):
            for zlo in range(4):
                place = jnp.where(south, 3 - zlo, zlo) * (8 * 264) + 2 * pair + b
                row = b * 128 + zlo * 32
                even, odd = grid[row : row + 11], grid[row + 16 : row + 27]
                for o in range(8):
                    base = place + o * 264
                    lanes = slice(o * 128, o * 128 + 128)
                    t_ref[pl.ds(base, 11, stride=8), :] = even[:, lanes]
                    t_ref[pl.ds(base + 88, 11, stride=8), :] = odd[:, lanes]
                    lanes = slice(1024 + o // 2 * 128, 1152 + o // 2 * 128)
                    first, last = even[:, lanes], odd[:, lanes]
                    if o % 2 == 0:
                        tail = jnp.where(low, first, pltpu.roll(last, 64, 1))
                    else:
                        tail = jnp.where(low, pltpu.roll(first, 64, 1), last)
                    t_ref[pl.ds(base + 176, 11, stride=8), :] = tail
        return 0

    lax.fori_loop(0, 4, one, 0)
    o_ref[...] = t_ref[...].reshape(32, 264, 128).astype(BF16)


def inverse(position, pieces, table):
    return call(
        inverse_kernel,
        jax.ShapeDtypeStruct((32, 264, 128), BF16),
        [position, *pieces, table],
        scratch=[pltpu.VMEM((6144, 128), F32), pltpu.VMEM((32 * 264, 128), F32)],
        specs=[SMEM] + [None] * 9,
        us=9,
        name="inverse",
    )


def finish_kernel(p_ref, r_ref, g_ref, o_ref, s_ref):
    south = p_ref[0] >= 4
    s_ref[...] = r_ref[...].astype(F32)
    for pair in range(11):
        row = 176 + pair * 8
        tail = s_ref[:, row : row + 8, :].reshape(CH, 128).T
        for parity in range(2):
            j = 2 * pair + parity
            j = jnp.where(south, 21 - j, j)
            row = (parity * 11 + pair) * 8
            head = s_ref[:, row : row + 8, :].reshape(CH, 128).T
            o_ref[j, 0:128, :] = (g_ref[j, 0:128, :].astype(F32) + head).astype(BF16)
            rest = tail[parity * 64 : parity * 64 + 52]
            o_ref[j, 128:180, :] = (g_ref[j, 128:180, :].astype(F32) + rest).astype(BF16)


def finish(position, received, cotangent):
    return call(
        finish_kernel,
        jax.ShapeDtypeStruct((ROWS, POINTS, CH), BF16),
        [position, received, cotangent],
        scratch=[pltpu.VMEM((32, 264, 128), F32)],
        specs=[SMEM, None, None],
        us=4,
        name="finish",
    )


def swap(value):
    return lax.all_to_all(value, RING, split_axis=0, concat_axis=0, tiled=True)


def cross(pieces):
    moved = [pieces[0]]
    for k in range(1, 8):
        pairs = [(p, partner(p, k)[0]) for p in range(8)]
        moved.append(lax.ppermute(pieces[k], CROSS, pairs))
    return moved


def along_y(value, width, axis):
    y = lax.axis_index("y")
    out = None
    for step in range(4):
        piece = lax.dynamic_slice_in_dim(value, (y + step) % 4 * width, width, axis)
        if step > 0:
            piece = lax.ppermute(piece, "y", [(i, (i + step) % 4) for i in range(4)])
        if out is None:
            out = jnp.zeros((4, *piece.shape), piece.dtype)
        out = lax.dynamic_update_index_in_dim(out, piece, (y + 4 - step) % 4, 0)
    return out


def after(value, *others):
    return lax.optimization_barrier((value, *others))[0]


def slot_rows():
    slot = jnp.arange(512, dtype=jnp.int32)
    device, within = slot // 128, slot % 128
    zlo, parity, pair = within // 32, within % 32 // 16, within % 16
    row = (device // 2) * 176 + zlo * 44 + (device % 2) * 22 + 2 * pair + parity
    mirrored = (NLAT - 1 - row).reshape(4, 128)[::-1].reshape(512)
    valid = pair < 11
    return jnp.concatenate([row, mirrored]), jnp.concatenate([valid, valid])


def local(grid_input, cotangent, mixing):
    position = lax.axis_index("x") * 2 + lax.axis_index("core")
    where = jnp.full((1,), position, jnp.int32)
    packed_g = pack(where, cotangent)
    sent_g = swap(packed_g)
    packed_x = pack(where, after(grid_input, packed_g))
    turn = [(0, 0), (1, 2), (2, 1), (3, 3)]
    mixing = after(mixing, packed_g)
    weights = jnp.transpose(along_y(mixing, 3, 0), (1, 0, 2, 3)).reshape(3, 128, CH)
    weights = lax.ppermute(weights, ("core", "zhi"), turn)
    row, valid = slot_rows()
    colatitude = (row.astype(F32) + 0.5) * (math.pi / NLAT)
    sine = jnp.sin(colatitude)
    quadrature = jnp.where(valid, math.pi / NLAT * sine, 0.0)
    cosine = jnp.where(valid, jnp.cos(colatitude), 0.0)[0:512]
    orders = 8 * jnp.arange(48, dtype=jnp.int32) + position
    order_value = orders.astype(F32)[:, None]
    counter = jnp.arange(1, ORDERS + 1, dtype=F32)[None, :]
    log_terms = jnp.where(counter <= order_value, jnp.log1p(0.5 / counter), 0.0)
    logs = (
        0.5 * math.log(0.5)
        + 0.5 * jnp.sum(log_terms, axis=1, keepdims=True)
        + order_value * jnp.log(sine[0:512])[None, :]
    )
    logs = jnp.where(valid[None, 0:512], logs, -1e30)
    table = legendre_table(
        after(jnp.broadcast_to(order_value, (48, 128)), packed_x),
        jnp.broadcast_to(cosine[None, :], (8, 512)),
        logs,
    )
    forward, backward = fourier_tables()
    own = lax.dynamic_slice_in_dim(quadrature, position * 128, 128)
    sent_g = after(sent_g, table, packed_x, forward, backward, weights)
    sent_x = swap(after(packed_x, sent_g))
    weights = lax.all_gather(after(weights, sent_g), CROSS, axis=0, tiled=False)
    weights = weights.reshape(4, 2, 3, 128, CH)
    pieces_g = fourier(where, sent_g, backward, jnp.ones((8, 128), F32))
    adjoint = swap(analyse(where, cross(pieces_g), table))
    pieces_x = fourier(where, sent_x, forward, jnp.broadcast_to(own[None, :], (8, 128)))
    mixed = swap(mix(adjoint, weights))
    coefficients = analyse(where, cross(pieces_x), table)
    coefficients = swap(after(coefficients, mixed))
    back = synthesise(where, mixed, table, jnp.broadcast_to(quadrature[None, :], (8, 1024)))
    grid_back = swap(inverse(where, cross(back), forward))
    partial = weight_sums(after(coefficients, *back), adjoint).reshape(8, 3, 128, CH)
    total = lax.psum_scatter(partial, CROSS, scatter_dimension=0, tiled=True).reshape(3, 128, CH)
    total = along_y(total, 32, 1).reshape(12, 32, CH)
    weight_grad = lax.ppermute(total, ("core", "zhi"), turn)
    return finish(where, grid_back, cotangent), weight_grad


def solution(mesh):
    fine = Mesh(mesh.devices.reshape(4, 4, 2, 2, 4), ("x", "zlo", "core", "zhi", "y"))
    spec = P(("x", "zlo", "core"), ("zhi", "y"), None)
    return jax.shard_map(
        local, mesh=fine, in_specs=(spec, spec, spec), out_specs=(spec, spec), check_vma=False
    )
```

```python
import math

import jax
import jax.numpy as jnp
from jax import lax
from jax.experimental import pallas as pl
from jax.experimental.pallas import tpu as pltpu
from jax.sharding import Mesh, PartitionSpec as P

F32 = jnp.float32
BF16 = jnp.bfloat16
NLON, NLAT, ORDERS, DEGREES = 1440, 704, 384, 384
ROWS, POINTS, CH = 22, 180, 256
RING = ("zlo", "zhi", "y")
CROSS = ("x", "core")
NT = (((1,), (1,)), ((), ()))
TN = (((0,), (0,)), ((), ()))
SMEM = pl.BlockSpec(memory_space=pltpu.SMEM)
PIECE = jax.ShapeDtypeStruct((768, 128), BF16)


def call(body, outs, ins, grid=(1,), scratch=(), us=1, specs=None, out_specs=None, name=None):
    whole = lambda a: pl.BlockSpec(a.shape, lambda *_, n=len(a.shape): (0,) * n)
    specs = specs or [None] * len(ins)
    return pl.pallas_call(
        body,
        out_shape=outs,
        grid=grid,
        in_specs=[whole(a) if s is None else s for a, s in zip(ins, specs)],
        out_specs=out_specs or jax.tree.map(whole, outs),
        scratch_shapes=list(scratch),
        compiler_params=pltpu.CompilerParams(vmem_limit_bytes=56 * 2**20),
        cost_estimate=pl.CostEstimate(
            flops=us * 1_100_000_000, bytes_accessed=us * 1_000_000, transcendentals=0
        ),
        name=name,
    )(*ins)


def partner(position, k):
    dx, dc = divmod(k, 2)
    x, core = position // 2, position % 2
    core = (core + dc) % 2
    return ((x + dx) % 4) * 2 + core, ((x + 4 - dx) % 4) * 2 + core


def pack_kernel(p_ref, x_ref, o_ref, s_ref):
    south = p_ref[0] >= 4
    eye = (
        lax.broadcasted_iota(jnp.int32, (CH, CH), 0) == lax.broadcasted_iota(jnp.int32, (CH, CH), 1)
    ).astype(BF16)
    zeros = jnp.zeros((CH, 76), F32)
    for pair in range(11):
        tail = None
        for parity in range(2):
            j = 2 * pair + parity
            j = jnp.where(south, 21 - j, j)
            head = lax.dot_general(eye, x_ref[j, 0:128, :], NT, preferred_element_type=F32)
            row = (parity * 11 + pair) * 8
            s_ref[:, row : row + 8, :] = head.reshape(32, 8, 128)
            rest = lax.dot_general(eye, x_ref[j, 128:180, :], NT, preferred_element_type=F32)
            rest = jnp.concatenate([rest, zeros], axis=1)
            tail = rest if parity == 0 else tail + pltpu.roll(rest, 64, 1)
        row = 176 + pair * 8
        s_ref[:, row : row + 8, :] = tail.reshape(32, 8, 128)
    o_ref[...] = s_ref[...].astype(BF16)


def pack(position, x):
    return call(
        pack_kernel,
        jax.ShapeDtypeStruct((32, 264, 128), BF16),
        [position, x],
        scratch=[pltpu.VMEM((32, 264, 128), F32)],
        specs=[SMEM, None],
        us=5,
        name="pack",
    )


def waves_kernel(c_ref, s_ref, f_ref, b_ref):
    for d in range(8):
        rows = slice(d * 96, d * 96 + 96)
        order = 8 * (lax.broadcasted_iota(jnp.int32, (96, 128), 0) // 2) + d
        factor = jnp.where(order == 0, 1.0 / NLON, 2.0 / NLON)
        low = lax.broadcasted_iota(jnp.int32, (96, 128), 1) < 64

        def turned(o, lanes):
            angle = (d * o) % 8 * math.pi / 4
            return c_ref[rows, lanes] * math.cos(angle) - s_ref[rows, lanes] * math.sin(angle)

        def put(value, place):
            f_ref[rows, place * 128 : place * 128 + 128] = value.astype(BF16)
            b_ref[rows, place * 128 : place * 128 + 128] = (value * factor).astype(BF16)

        for o in range(8):
            put(turned(o, slice(0, 128)), o)
        for o in range(4):
            tails = [turned(2 * o + i, slice(128, 256)) for i in range(2)]
            put(jnp.where(low, tails[0], tails[1]), 8 + o)


def fourier_tables():
    q = jnp.arange(768, dtype=jnp.int32)
    order, quarter = 8 * (q % 96 // 2) + q // 96, q % 2
    lane = jnp.arange(256, dtype=jnp.int32)
    point = jnp.where(lane < 128, lane, 128 + lane % 64)
    valid = (point < POINTS)[None, :]
    phase = (point[None, :] * order[:, None] + 360 * quarter[:, None]) % NLON
    angle = phase.astype(F32) * (2.0 * math.pi / NLON)
    table = jax.ShapeDtypeStruct((768, 1536), BF16)
    return call(
        waves_kernel,
        (table, table),
        [jnp.where(valid, jnp.cos(angle), 0.0), jnp.where(valid, jnp.sin(angle), 0.0)],
        us=4,
        name="waves",
    )


def fourier_kernel(p_ref, r_ref, f_ref, w_ref, *refs):
    o_refs, (s_ref, k_ref, t_ref) = refs[:8], refs[8:]
    position = p_ref[0]
    south = position >= 4
    s_ref[0 : 32 * 264, :] = r_ref[...].reshape(32 * 264, 128).astype(F32)
    s_ref[32 * 264 :, :] = jnp.zeros((64, 128), F32)
    low = lax.broadcasted_iota(jnp.int32, (16, 128), 1) < 64

    def one(pair, _):
        for b in range(2):
            c = 2 * pair + b
            for zlo in range(4):
                source = jnp.where(south, 3 - zlo, zlo) * (8 * 264) + c
                row = b * 128 + zlo * 32
                tails = []
                for o in range(8):
                    base = source + o * 264
                    for parity in range(2):
                        k_ref[row + parity * 16 : row + parity * 16 + 16, o * 128 : o * 128 + 128] = (
                            s_ref[pl.ds(base + parity * 88, 16, stride=8), :].astype(BF16)
                        )
                    tails.append(s_ref[pl.ds(base + 176, 16, stride=8), :])
                for o in range(4):
                    even, odd = tails[2 * o], tails[2 * o + 1]
                    lanes = slice(1024 + o * 128, 1152 + o * 128)
                    north = jnp.where(low, even, pltpu.roll(odd, 64, 1))
                    k_ref[row : row + 16, lanes] = north.astype(BF16)
                    other = jnp.where(low, pltpu.roll(even, 64, 1), odd)
                    k_ref[row + 16 : row + 32, lanes] = other.astype(BF16)
        spec = lax.dot_general(f_ref[...], k_ref[...], NT, preferred_element_type=F32)
        for b in range(2):
            value = spec[:, b * 128 : b * 128 + 128] * w_ref[0:1, :]
            t_ref[pl.ds(2 * pair + b, 768, stride=8), :] = value
        return 0

    lax.fori_loop(0, 4, one, 0)
    for k in range(8):
        start = pl.multiple_of(partner(position, k)[0] * 768, 768)
        o_refs[k][...] = t_ref[pl.ds(start, 768), :].astype(BF16)


def fourier(position, received, table, weights):
    return call(
        fourier_kernel,
        (PIECE,) * 8,
        [position, received, table, weights],
        scratch=[
            pltpu.VMEM((32 * 264 + 64, 128), F32),
            pltpu.VMEM((256, 1536), BF16),
            pltpu.VMEM((6144, 128), F32),
        ],
        specs=[SMEM, None, None, None],
        us=9,
        name="fourier",
    )


def block_orders(i):
    return jnp.where(i < 6, i // 3, jnp.where(i < 10, 2 + (i - 6) // 2, i - 6))


def block_degrees(i):
    return jnp.where(i < 6, i % 3, jnp.where(i < 10, 1 + i % 2, 2))


def table_kernel(m_ref, cos_ref, log_ref, o_ref, s_ref, v_ref):
    i = pl.program_id(0)
    group, part = block_orders(i), block_degrees(i)

    @pl.when(part == group // 2)
    def _():
        v_ref[0] = jnp.zeros((8, 512), F32)
        v_ref[1] = jnp.zeros((8, 512), F32)
        v_ref[2] = log_ref[...]

    order = m_ref[...]
    square = order * order
    cosine = cos_ref[...]
    wide = lambda a: jnp.concatenate([a] * 4, axis=1)

    def steps(n, carried):
        previous, earlier, scale = carried
        size = jnp.exp(scale)
        for u in range(8):
            l = n * 8 + u
            degree = jnp.full((8, 128), part * 128 + l, jnp.int32).astype(F32)
            below = (degree - 1.0) * (degree - 1.0)
            growth = jnp.sqrt(
                jnp.maximum(4.0 * degree * degree - 1.0, 0.0)
                / jnp.maximum(degree * degree - square, 1.0)
            )
            shrink = jnp.sqrt(
                jnp.maximum(below - square, 0.0) / jnp.maximum(4.0 * below - 1.0, 1.0)
            )
            current = wide(growth) * (cosine * previous) - wide(growth * shrink) * earlier
            current = jnp.where(wide(degree == order), 1.0, current)
            value = current * size
            for d in range(4):
                s_ref[d, pl.ds(pl.multiple_of(l * 8, 8), 8), :] = value[:, d * 128 : d * 128 + 128]
            previous, earlier = current, previous
        over = jnp.maximum(jnp.abs(previous), jnp.abs(earlier)) > 1e5
        factor = jnp.where(over, 1e-10, 1.0)
        scale = scale + jnp.where(over, math.log(1e10), 0.0)
        return previous * factor, earlier * factor, scale

    state = lax.fori_loop(0, 16, steps, (v_ref[0], v_ref[1], v_ref[2]))
    for n in range(3):
        v_ref[n] = state[n]
    for s in range(8):
        for d in range(4):
            o_ref[0, s, :, d * 128 : d * 128 + 128] = s_ref[
                d, pl.ds(s, 128, stride=8), :
            ].astype(BF16)


def legendre_table(orders, cosine, logs):
    return call(
        table_kernel,
        jax.ShapeDtypeStruct((12, 8, 128, 512), BF16),
        [orders, cosine, logs],
        grid=(12,),
        scratch=[pltpu.VMEM((4, 1024, 128), F32), pltpu.VMEM((3, 8, 512), F32)],
        specs=[
            pl.BlockSpec((8, 128), lambda i: (block_orders(i), 0)),
            None,
            pl.BlockSpec((8, 512), lambda i: (block_orders(i), 0)),
        ],
        out_specs=pl.BlockSpec((1, 8, 128, 512), lambda i: (i, 0, 0, 0)),
        us=25,
        name="legendre",
    )


def pick(g, *values):
    out = values[-1]
    for n in reversed(range(len(values) - 1)):
        out = jnp.where(g == n, values[n], out)
    return out


TABLE = [
    pl.BlockSpec((1, 8, 128, 512), lambda g, v=v: (pick(g, *v), 0, 0, 0))
    for v in ((0, 3), (1, 4, 6, 8), (2, 5, 7, 9, 10, 11))
]


def by_parts(group, body):
    for first in range(3):

        @pl.when(group // 2 == first)
        def _(first=first):
            body(first)


def signs(position, rows):
    lane = lax.broadcasted_iota(jnp.int32, (rows, 128), 1)
    return jnp.where((lane + position) % 2 == 0, 1.0, -1.0)


def analyse_kernel(p_ref, *refs):
    pieces, t_refs, (o_ref, s_ref, c_ref, q_ref) = refs[:8], refs[8:11], refs[11:]
    group = pl.program_id(0)
    position = p_ref[0]

    @pl.when(group == 0)
    def _():
        for k in range(8):
            s_ref[partner(position, k)[1]] = pieces[k][...]
        c_ref[...] = jnp.zeros_like(c_ref)

    sign = signs(position, 16)

    def body(first):
        for s in range(8):
            row = pl.multiple_of(group * 128 + s * 16, 16)
            north = jnp.concatenate([s_ref[d, pl.ds(row, 16), :] for d in range(4)], axis=1)
            south = jnp.concatenate([s_ref[7 - d, pl.ds(row, 16), :] for d in range(4)], axis=1)
            value = lax.dot_general(
                jnp.concatenate([north, south], axis=0),
                jnp.concatenate([t_refs[b][0, s] for b in range(first, 3)], axis=0),
                NT,
                preferred_element_type=F32,
            )
            for b in range(first, 3):
                lanes = slice((b - first) * 128, (b - first) * 128 + 128)
                c_ref[b, pl.ds(row, 16), :] = value[0:16, lanes] + sign * value[16:32, lanes]

    by_parts(group, body)

    @pl.when(group == 5)
    def _():
        lane = lax.broadcasted_iota(jnp.int32, (96, 128), 1)
        for c in range(8):
            block = jnp.concatenate(
                [c_ref[b, pl.ds(c, 96, stride=8), :] for b in range(3)], axis=1
            )
            block = jnp.concatenate([block, jnp.zeros((32, DEGREES), F32)], axis=0).T
            first = jnp.where(lane < 96, block[288:384], pltpu.roll(block[0:96], 96, 1))
            second = jnp.where(lane < 72, block[192:288], pltpu.roll(block[96:192], 72, 1))
            q_ref[0, pl.ds(c, 96, stride=8), :] = first
            q_ref[1, pl.ds(c, 96, stride=8), :] = second
        o_ref[...] = jnp.concatenate(
            [q_ref[0].reshape(32, 24, 128), q_ref[1].reshape(32, 24, 128)], axis=1
        ).astype(BF16)


def analyse(position, pieces, table):
    return call(
        analyse_kernel,
        jax.ShapeDtypeStruct((32, 48, 128), BF16),
        [position, *pieces, table, table, table],
        grid=(6,),
        scratch=[
            pltpu.VMEM((8, 768, 128), BF16),
            pltpu.VMEM((3, 768, 128), F32),
            pltpu.VMEM((2, 768, 128), F32),
        ],
        specs=[SMEM] + [None] * 8 + TABLE,
        us=10,
        name="analyse",
    )


def pair_rows(ref, p):
    return ref[:, p * 8 : p * 8 + 8, :].astype(F32).reshape(CH, 128).astype(BF16)


def mix_kernel(a_ref, w_ref, o_ref):
    lane = lax.broadcasted_iota(jnp.int32, (CH, 128), 1)
    pieces = []
    for p in range(6):
        half, e = divmod(p, 3)
        rows = pair_rows(a_ref, p)
        high = jnp.dot(w_ref[3 - half, :, e].reshape(CH, CH), rows, preferred_element_type=F32)
        low = jnp.dot(w_ref[half, :, e].reshape(CH, CH), rows, preferred_element_type=F32)
        pieces.append(jnp.where(lane < 96 - 24 * half, high, low).reshape(32, 8, 128))
    o_ref[...] = jnp.concatenate(pieces, axis=1).astype(BF16)


def mix(adjoint, mixing):
    return call(
        mix_kernel,
        jax.ShapeDtypeStruct((32, 48, 128), BF16),
        [adjoint, mixing],
        us=3,
        name="mix",
    )


PART = jax.ShapeDtypeStruct((3, 128, CH), F32)


def grad_kernel(p_ref, c_ref, a_ref, *refs):
    o_refs, s_ref = refs[:8], refs[8]
    lane = lax.broadcasted_iota(jnp.int32, (CH, 128), 1)
    for p in range(6):
        half, e = divmod(p, 3)
        left, right = pair_rows(c_ref, p), pair_rows(a_ref, p)
        inside = lane < 96 - 24 * half
        zero = jnp.zeros_like(left)
        high = lax.dot_general(jnp.where(inside, left, zero), right, NT, preferred_element_type=F32)
        low = lax.dot_general(jnp.where(inside, zero, left), right, NT, preferred_element_type=F32)
        for n in range(2):
            s_ref[2 * (3 - half) + n, e] = high[n * 128 : n * 128 + 128]
            s_ref[2 * half + n, e] = low[n * 128 : n * 128 + 128]
    for k in range(8):
        o_refs[k][...] = s_ref[partner(p_ref[0], k)[0]]


def weight_sums(position, coefficients, adjoint):
    return call(
        grad_kernel,
        (PART,) * 8,
        [position, coefficients, adjoint],
        scratch=[pltpu.VMEM((8, 3, 128, CH), F32)],
        specs=[SMEM, None, None],
        us=4,
        name="grad",
    )


def total_kernel(y_ref, *refs):
    pieces, o_refs, s_ref = refs[:8], refs[8:12], refs[12]
    total = pieces[0][...]
    for k in range(1, 8):
        total = total + pieces[k][...]
    s_ref[...] = total
    for step in range(4):
        row = pl.multiple_of((y_ref[0] + step) % 4 * 32, 32)
        o_refs[step][...] = s_ref[:, pl.ds(row, 32), :]


def total_sums(y, pieces):
    return call(
        total_kernel,
        (jax.ShapeDtypeStruct((3, 32, CH), F32),) * 4,
        [y, *pieces],
        scratch=[pltpu.VMEM((3, 128, CH), F32)],
        specs=[SMEM] + [None] * 8,
        us=3,
        name="total",
    )


def gather_kernel(p_ref, *refs):
    for k in range(8):
        refs[8][partner(p_ref[0], k)[1]] = refs[k][...]


def gather(position, pieces):
    return call(
        gather_kernel,
        jax.ShapeDtypeStruct((8, 3, 128, CH), BF16),
        [position, *pieces],
        specs=[SMEM] + [None] * 8,
        us=2,
        name="gather",
    )


def synthesise_kernel(p_ref, m_ref, w_ref, *refs):
    t_refs, o_refs, (q_ref, c_ref, b_ref) = refs[:3], refs[3:11], refs[11:]
    group = pl.program_id(0)
    position = p_ref[0]

    @pl.when(group == 0)
    def _():
        mixed = m_ref[...].astype(F32)
        q_ref[0] = mixed[:, 0:24, :].reshape(768, 128)
        q_ref[1] = mixed[:, 24:48, :].reshape(768, 128)
        for c in range(8):
            first = q_ref[0, pl.ds(c, 96, stride=8), :]
            second = q_ref[1, pl.ds(c, 96, stride=8), :]
            block = jnp.concatenate(
                [pltpu.roll(first, 32, 1), pltpu.roll(second, 56, 1), second, first], axis=0
            )
            block = block.T[0:96, :]
            for b in range(3):
                c_ref[b, pl.ds(c, 96, stride=8), :] = block[:, b * 128 : b * 128 + 128]

    sign = signs(position, 16)

    def body(first):
        for s in range(8):
            row = pl.multiple_of(group * 128 + s * 16, 16)
            north = [c_ref[b, pl.ds(row, 16), :] for b in range(first, 3)]
            south = [a * sign for a in north]
            left = jnp.concatenate(
                [jnp.concatenate(north, axis=1), jnp.concatenate(south, axis=1)], axis=0
            ).astype(BF16)
            right = jnp.concatenate([t_refs[b][0, s] for b in range(first, 3)], axis=0)
            value = jnp.dot(left, right, preferred_element_type=F32)
            for d in range(4):
                lanes = slice(d * 128, d * 128 + 128)
                mirror = slice((7 - d) * 128, (7 - d) * 128 + 128)
                b_ref[d, pl.ds(row, 16), :] = (value[0:16, lanes] * w_ref[0:1, lanes]).astype(BF16)
                b_ref[7 - d, pl.ds(row, 16), :] = (
                    value[16:32, lanes] * w_ref[0:1, mirror]
                ).astype(BF16)

    by_parts(group, body)

    @pl.when(group == 5)
    def _():
        for k in range(8):
            o_refs[k][...] = b_ref[partner(position, k)[0]]


def synthesise(position, mixed, table, weights):
    return call(
        synthesise_kernel,
        (PIECE,) * 8,
        [position, mixed, weights, table, table, table],
        grid=(6,),
        scratch=[
            pltpu.VMEM((2, 768, 128), F32),
            pltpu.VMEM((3, 768, 128), F32),
            pltpu.VMEM((8, 768, 128), BF16),
        ],
        specs=[SMEM, None, None] + TABLE,
        us=10,
        name="synthesise",
    )


def inverse_kernel(p_ref, *refs):
    pieces, (f_ref, o_ref, s_ref, t_ref) = refs[:8], refs[8:]
    position = p_ref[0]
    south = position >= 4
    for k in range(8):
        start = pl.multiple_of(partner(position, k)[1] * 768, 768)
        s_ref[pl.ds(start, 768), :] = pieces[k][...].astype(F32)
    low = lax.broadcasted_iota(jnp.int32, (11, 128), 1) < 64

    def one(pair, _):
        left = jnp.concatenate(
            [s_ref[pl.ds(2 * pair + b, 768, stride=8), :].astype(BF16) for b in range(2)], axis=1
        )
        grid = lax.dot_general(left, f_ref[...], TN, preferred_element_type=F32)
        for b in range(2):
            for zlo in range(4):
                place = jnp.where(south, 3 - zlo, zlo) * (8 * 264) + 2 * pair + b
                row = b * 128 + zlo * 32
                even, odd = grid[row : row + 11], grid[row + 16 : row + 27]
                for o in range(8):
                    base = place + o * 264
                    lanes = slice(o * 128, o * 128 + 128)
                    t_ref[pl.ds(base, 11, stride=8), :] = even[:, lanes]
                    t_ref[pl.ds(base + 88, 11, stride=8), :] = odd[:, lanes]
                    lanes = slice(1024 + o // 2 * 128, 1152 + o // 2 * 128)
                    first, last = even[:, lanes], odd[:, lanes]
                    if o % 2 == 0:
                        tail = jnp.where(low, first, pltpu.roll(last, 64, 1))
                    else:
                        tail = jnp.where(low, pltpu.roll(first, 64, 1), last)
                    t_ref[pl.ds(base + 176, 11, stride=8), :] = tail
        return 0

    lax.fori_loop(0, 4, one, 0)
    o_ref[...] = t_ref[...].reshape(32, 264, 128).astype(BF16)


def inverse(position, pieces, table):
    return call(
        inverse_kernel,
        jax.ShapeDtypeStruct((32, 264, 128), BF16),
        [position, *pieces, table],
        scratch=[pltpu.VMEM((6144, 128), F32), pltpu.VMEM((32 * 264, 128), F32)],
        specs=[SMEM] + [None] * 9,
        us=9,
        name="inverse",
    )


def finish_kernel(p_ref, r_ref, g_ref, o_ref, s_ref):
    south = p_ref[0] >= 4
    s_ref[...] = r_ref[...].astype(F32)
    for pair in range(11):
        row = 176 + pair * 8
        tail = s_ref[:, row : row + 8, :].reshape(CH, 128).T
        for parity in range(2):
            j = 2 * pair + parity
            j = jnp.where(south, 21 - j, j)
            row = (parity * 11 + pair) * 8
            head = s_ref[:, row : row + 8, :].reshape(CH, 128).T
            o_ref[j, 0:128, :] = (g_ref[j, 0:128, :].astype(F32) + head).astype(BF16)
            rest = tail[parity * 64 : parity * 64 + 52]
            o_ref[j, 128:180, :] = (g_ref[j, 128:180, :].astype(F32) + rest).astype(BF16)


def finish(position, received, cotangent):
    return call(
        finish_kernel,
        jax.ShapeDtypeStruct((ROWS, POINTS, CH), BF16),
        [position, received, cotangent],
        scratch=[pltpu.VMEM((32, 264, 128), F32)],
        specs=[SMEM, None, None],
        us=4,
        name="finish",
    )


def swap(value):
    return lax.all_to_all(value, RING, split_axis=0, concat_axis=0, tiled=True)


def cross(pieces):
    moved = [pieces[0]]
    for k in range(1, 8):
        pairs = [(p, partner(p, k)[0]) for p in range(8)]
        moved.append(lax.ppermute(pieces[k], CROSS, pairs))
    return moved


def turned(pieces):
    moved = []
    for step, piece in enumerate(pieces):
        pairs = [
            (core * 8 + zhi * 4 + y, zhi * 8 + core * 4 + (y + step) % 4)
            for core in range(2)
            for zhi in range(2)
            for y in range(4)
        ]
        moved.append(lax.ppermute(piece, ("core", "zhi", "y"), pairs))
    y = lax.axis_index("y")
    out = jnp.zeros((4, *pieces[0].shape), pieces[0].dtype)
    for step, piece in enumerate(moved):
        out = lax.dynamic_update_index_in_dim(out, piece, (y + 4 - step) % 4, 0)
    return out


def after(value, *others):
    return lax.optimization_barrier((value, *others))[0]


def slot_rows():
    slot = jnp.arange(512, dtype=jnp.int32)
    device, within = slot // 128, slot % 128
    zlo, parity, pair = within // 32, within % 32 // 16, within % 16
    row = (device // 2) * 176 + zlo * 44 + (device % 2) * 22 + 2 * pair + parity
    mirrored = (NLAT - 1 - row).reshape(4, 128)[::-1].reshape(512)
    valid = pair < 11
    return jnp.concatenate([row, mirrored]), jnp.concatenate([valid, valid])


def local(grid_input, cotangent, mixing):
    position = lax.axis_index("x") * 2 + lax.axis_index("core")
    y = lax.axis_index("y")
    where = jnp.full((1,), position, jnp.int32)
    packed_g = pack(where, cotangent)
    weights = turned(
        [lax.dynamic_slice_in_dim(mixing, (y + step) % 4 * 3, 3, 0) for step in range(4)]
    )
    sent_g = swap(after(packed_g, weights))
    weights = jnp.transpose(weights, (1, 0, 2, 3)).reshape(3, 128, CH)
    weights = gather(where, cross([after(weights, packed_g)] * 8)).reshape(4, 2, 3, 128, CH)
    packed_x = pack(where, after(grid_input, packed_g))
    row, valid = slot_rows()
    colatitude = (row.astype(F32) + 0.5) * (math.pi / NLAT)
    sine = jnp.sin(colatitude)
    quadrature = jnp.where(valid, math.pi / NLAT * sine, 0.0)
    cosine = jnp.where(valid, jnp.cos(colatitude), 0.0)[0:512]
    orders = 8 * jnp.arange(48, dtype=jnp.int32) + position
    order_value = orders.astype(F32)[:, None]
    counter = jnp.arange(1, ORDERS + 1, dtype=F32)[None, :]
    log_terms = jnp.where(counter <= order_value, jnp.log1p(0.5 / counter), 0.0)
    logs = (
        0.5 * math.log(0.5)
        + 0.5 * jnp.sum(log_terms, axis=1, keepdims=True)
        + order_value * jnp.log(sine[0:512])[None, :]
    )
    logs = jnp.where(valid[None, 0:512], logs, -1e30)
    forward, backward = fourier_tables()
    own = lax.dynamic_slice_in_dim(quadrature, position * 128, 128)
    sent_g = after(sent_g, packed_x, forward, backward, weights)
    sent_x = swap(after(packed_x, sent_g))
    pieces_g = fourier(where, sent_g, backward, jnp.ones((8, 128), F32))
    table = legendre_table(
        after(jnp.broadcast_to(order_value, (48, 128)), pieces_g[0]),
        jnp.broadcast_to(cosine[None, :], (8, 512)),
        logs,
    )
    adjoint = swap(after(analyse(where, cross(pieces_g), table), sent_x))
    pieces_x = fourier(where, sent_x, forward, jnp.broadcast_to(own[None, :], (8, 128)))
    mixed = swap(mix(after(adjoint, pieces_x[0]), weights))
    coefficients = analyse(where, cross(pieces_x), table)
    mixed = after(mixed, coefficients)
    back = synthesise(where, mixed, table, jnp.broadcast_to(quadrature[None, :], (8, 1024)))
    coefficients = swap(after(coefficients, back[0]))
    packed_back = inverse(where, cross(back), forward)
    grid_back = swap(packed_back)
    partial = weight_sums(where, coefficients, adjoint)
    total = total_sums(jnp.full((1,), y, jnp.int32), cross(after(partial, packed_back)))
    weight_grad = turned(total).reshape(12, 32, CH)
    return finish(where, grid_back, cotangent), weight_grad


def solution(mesh):
    fine = Mesh(mesh.devices.reshape(4, 4, 2, 2, 4), ("x", "zlo", "core", "zhi", "y"))
    spec = P(("x", "zlo", "core"), ("zhi", "y"), None)
    return jax.shard_map(
        local, mesh=fine, in_specs=(spec, spec, spec), out_specs=(spec, spec), check_vma=False
    )
```

```python
import math

import jax
import jax.numpy as jnp
from jax import lax
from jax.experimental import pallas as pl
from jax.experimental.pallas import tpu as pltpu
from jax.sharding import Mesh, PartitionSpec as P

F32 = jnp.float32
BF16 = jnp.bfloat16
NLON, NLAT, ORDERS, DEGREES = 1440, 704, 384, 384
ROWS, POINTS, CH = 22, 180, 256
RING = ("zlo", "zhi", "y")
CROSS = ("x", "core")
NT = (((1,), (1,)), ((), ()))
TN = (((0,), (0,)), ((), ()))
SMEM = pl.BlockSpec(memory_space=pltpu.SMEM)
PIECE = jax.ShapeDtypeStruct((768, 128), BF16)


def call(body, outs, ins, grid=(1,), scratch=(), us=1, specs=None, out_specs=None, name=None):
    whole = lambda a: pl.BlockSpec(a.shape, lambda *_, n=len(a.shape): (0,) * n)
    specs = specs or [None] * len(ins)
    return pl.pallas_call(
        body,
        out_shape=outs,
        grid=grid,
        in_specs=[whole(a) if s is None else s for a, s in zip(ins, specs)],
        out_specs=out_specs or jax.tree.map(whole, outs),
        scratch_shapes=list(scratch),
        compiler_params=pltpu.CompilerParams(vmem_limit_bytes=56 * 2**20),
        cost_estimate=pl.CostEstimate(
            flops=us * 1_100_000_000, bytes_accessed=us * 1_000_000, transcendentals=0
        ),
        name=name,
    )(*ins)


def partner(position, k):
    dx, dc = divmod(k, 2)
    x, core = position // 2, position % 2
    core = (core + dc) % 2
    return ((x + dx) % 4) * 2 + core, ((x + 4 - dx) % 4) * 2 + core


def pack_kernel(p_ref, x_ref, o_ref, s_ref):
    south = p_ref[0] >= 4
    eye = (
        lax.broadcasted_iota(jnp.int32, (CH, CH), 0) == lax.broadcasted_iota(jnp.int32, (CH, CH), 1)
    ).astype(BF16)
    zeros = jnp.zeros((CH, 76), F32)
    for pair in range(11):
        tail = None
        for parity in range(2):
            j = 2 * pair + parity
            j = jnp.where(south, 21 - j, j)
            head = lax.dot_general(eye, x_ref[j, 0:128, :], NT, preferred_element_type=F32)
            row = (parity * 11 + pair) * 8
            s_ref[:, row : row + 8, :] = head.reshape(32, 8, 128)
            rest = lax.dot_general(eye, x_ref[j, 128:180, :], NT, preferred_element_type=F32)
            rest = jnp.concatenate([rest, zeros], axis=1)
            tail = rest if parity == 0 else tail + pltpu.roll(rest, 64, 1)
        row = 176 + pair * 8
        s_ref[:, row : row + 8, :] = tail.reshape(32, 8, 128)
    o_ref[...] = s_ref[...].astype(BF16)


def pack(position, x):
    return call(
        pack_kernel,
        jax.ShapeDtypeStruct((32, 264, 128), BF16),
        [position, x],
        scratch=[pltpu.VMEM((32, 264, 128), F32)],
        specs=[SMEM, None],
        us=5,
        name="pack",
    )


def waves_kernel(c_ref, s_ref, f_ref, b_ref):
    for d in range(8):
        rows = slice(d * 96, d * 96 + 96)
        order = 8 * (lax.broadcasted_iota(jnp.int32, (96, 128), 0) // 2) + d
        factor = jnp.where(order == 0, 1.0 / NLON, 2.0 / NLON)
        low = lax.broadcasted_iota(jnp.int32, (96, 128), 1) < 64

        def turned(o, lanes):
            angle = (d * o) % 8 * math.pi / 4
            return c_ref[rows, lanes] * math.cos(angle) - s_ref[rows, lanes] * math.sin(angle)

        def put(value, place):
            f_ref[rows, place * 128 : place * 128 + 128] = value.astype(BF16)
            b_ref[rows, place * 128 : place * 128 + 128] = (value * factor).astype(BF16)

        for o in range(8):
            put(turned(o, slice(0, 128)), o)
        for o in range(4):
            tails = [turned(2 * o + i, slice(128, 256)) for i in range(2)]
            put(jnp.where(low, tails[0], tails[1]), 8 + o)


def fourier_tables():
    q = jnp.arange(768, dtype=jnp.int32)
    order, quarter = 8 * (q % 96 // 2) + q // 96, q % 2
    lane = jnp.arange(256, dtype=jnp.int32)
    point = jnp.where(lane < 128, lane, 128 + lane % 64)
    valid = (point < POINTS)[None, :]
    phase = (point[None, :] * order[:, None] + 360 * quarter[:, None]) % NLON
    angle = phase.astype(F32) * (2.0 * math.pi / NLON)
    table = jax.ShapeDtypeStruct((768, 1536), BF16)
    return call(
        waves_kernel,
        (table, table),
        [jnp.where(valid, jnp.cos(angle), 0.0), jnp.where(valid, jnp.sin(angle), 0.0)],
        us=4,
        name="waves",
    )


def fourier_kernel(p_ref, r_ref, f_ref, w_ref, *refs):
    o_refs, (s_ref, k_ref, t_ref) = refs[:8], refs[8:]
    position = p_ref[0]
    south = position >= 4
    s_ref[0 : 32 * 264, :] = r_ref[...].reshape(32 * 264, 128).astype(F32)
    s_ref[32 * 264 :, :] = jnp.zeros((64, 128), F32)
    low = lax.broadcasted_iota(jnp.int32, (16, 128), 1) < 64

    def one(pair, _):
        for b in range(2):
            c = 2 * pair + b
            for zlo in range(4):
                source = jnp.where(south, 3 - zlo, zlo) * (8 * 264) + c
                row = b * 128 + zlo * 32
                tails = []
                for o in range(8):
                    base = source + o * 264
                    for parity in range(2):
                        k_ref[row + parity * 16 : row + parity * 16 + 16, o * 128 : o * 128 + 128] = (
                            s_ref[pl.ds(base + parity * 88, 16, stride=8), :].astype(BF16)
                        )
                    tails.append(s_ref[pl.ds(base + 176, 16, stride=8), :])
                for o in range(4):
                    even, odd = tails[2 * o], tails[2 * o + 1]
                    lanes = slice(1024 + o * 128, 1152 + o * 128)
                    north = jnp.where(low, even, pltpu.roll(odd, 64, 1))
                    k_ref[row : row + 16, lanes] = north.astype(BF16)
                    other = jnp.where(low, pltpu.roll(even, 64, 1), odd)
                    k_ref[row + 16 : row + 32, lanes] = other.astype(BF16)
        spec = lax.dot_general(f_ref[...], k_ref[...], NT, preferred_element_type=F32)
        for b in range(2):
            value = spec[:, b * 128 : b * 128 + 128] * w_ref[0:1, :]
            t_ref[pl.ds(2 * pair + b, 768, stride=8), :] = value
        return 0

    lax.fori_loop(0, 4, one, 0)
    for k in range(8):
        start = pl.multiple_of(partner(position, k)[0] * 768, 768)
        o_refs[k][...] = t_ref[pl.ds(start, 768), :].astype(BF16)


def fourier(position, received, table, weights):
    return call(
        fourier_kernel,
        (PIECE,) * 8,
        [position, received, table, weights],
        scratch=[
            pltpu.VMEM((32 * 264 + 64, 128), F32),
            pltpu.VMEM((256, 1536), BF16),
            pltpu.VMEM((6144, 128), F32),
        ],
        specs=[SMEM, None, None, None],
        us=9,
        name="fourier",
    )


def block_orders(i):
    return jnp.where(i < 6, i // 3, jnp.where(i < 10, 2 + (i - 6) // 2, i - 6))


def block_degrees(i):
    return jnp.where(i < 6, i % 3, jnp.where(i < 10, 1 + i % 2, 2))


def table_kernel(m_ref, cos_ref, log_ref, o_ref, s_ref, v_ref):
    i = pl.program_id(0)
    group, part = block_orders(i), block_degrees(i)

    @pl.when(part == group // 2)
    def _():
        v_ref[0] = jnp.zeros((8, 512), F32)
        v_ref[1] = jnp.zeros((8, 512), F32)
        v_ref[2] = log_ref[...]

    order = m_ref[...]
    square = order * order
    cosine = cos_ref[...]
    wide = lambda a: jnp.concatenate([a] * 4, axis=1)

    def steps(n, carried):
        previous, earlier, scale = carried
        size = jnp.exp(scale)
        for u in range(8):
            l = n * 8 + u
            degree = jnp.full((8, 128), part * 128 + l, jnp.int32).astype(F32)
            below = (degree - 1.0) * (degree - 1.0)
            growth = jnp.sqrt(
                jnp.maximum(4.0 * degree * degree - 1.0, 0.0)
                / jnp.maximum(degree * degree - square, 1.0)
            )
            shrink = jnp.sqrt(
                jnp.maximum(below - square, 0.0) / jnp.maximum(4.0 * below - 1.0, 1.0)
            )
            current = wide(growth) * (cosine * previous) - wide(growth * shrink) * earlier
            current = jnp.where(wide(degree == order), 1.0, current)
            value = current * size
            for d in range(4):
                s_ref[d, pl.ds(pl.multiple_of(l * 8, 8), 8), :] = value[:, d * 128 : d * 128 + 128]
            previous, earlier = current, previous
        over = jnp.maximum(jnp.abs(previous), jnp.abs(earlier)) > 1e5
        factor = jnp.where(over, 1e-10, 1.0)
        scale = scale + jnp.where(over, math.log(1e10), 0.0)
        return previous * factor, earlier * factor, scale

    state = lax.fori_loop(0, 16, steps, (v_ref[0], v_ref[1], v_ref[2]))
    for n in range(3):
        v_ref[n] = state[n]
    for s in range(8):
        for d in range(4):
            o_ref[0, s, :, d * 128 : d * 128 + 128] = s_ref[
                d, pl.ds(s, 128, stride=8), :
            ].astype(BF16)


def legendre_table(orders, cosine, logs):
    return call(
        table_kernel,
        jax.ShapeDtypeStruct((12, 8, 128, 512), BF16),
        [orders, cosine, logs],
        grid=(12,),
        scratch=[pltpu.VMEM((4, 1024, 128), F32), pltpu.VMEM((3, 8, 512), F32)],
        specs=[
            pl.BlockSpec((8, 128), lambda i: (block_orders(i), 0)),
            None,
            pl.BlockSpec((8, 512), lambda i: (block_orders(i), 0)),
        ],
        out_specs=pl.BlockSpec((1, 8, 128, 512), lambda i: (i, 0, 0, 0)),
        us=25,
        name="legendre",
    )


def pick(g, *values):
    out = values[-1]
    for n in reversed(range(len(values) - 1)):
        out = jnp.where(g == n, values[n], out)
    return out


TABLE = [
    pl.BlockSpec((1, 8, 128, 512), lambda g, v=v: (pick(g, *v), 0, 0, 0))
    for v in ((0, 3), (1, 4, 6, 8), (2, 5, 7, 9, 10, 11))
]


def by_parts(group, body):
    for first in range(3):

        @pl.when(group // 2 == first)
        def _(first=first):
            body(first)


def signs(position, rows):
    lane = lax.broadcasted_iota(jnp.int32, (rows, 128), 1)
    return jnp.where((lane + position) % 2 == 0, 1.0, -1.0)


def analyse_kernel(p_ref, *refs):
    pieces, t_refs, (o_ref, s_ref, c_ref, q_ref) = refs[:8], refs[8:11], refs[11:]
    group = pl.program_id(0)
    position = p_ref[0]

    @pl.when(group == 0)
    def _():
        for k in range(8):
            s_ref[partner(position, k)[1]] = pieces[k][...]
        c_ref[...] = jnp.zeros_like(c_ref)

    sign = signs(position, 16)

    def body(first):
        for s in range(8):
            row = pl.multiple_of(group * 128 + s * 16, 16)
            north = jnp.concatenate([s_ref[d, pl.ds(row, 16), :] for d in range(4)], axis=1)
            south = jnp.concatenate([s_ref[7 - d, pl.ds(row, 16), :] for d in range(4)], axis=1)
            value = lax.dot_general(
                jnp.concatenate([north, south], axis=0),
                jnp.concatenate([t_refs[b][0, s] for b in range(first, 3)], axis=0),
                NT,
                preferred_element_type=F32,
            )
            for b in range(first, 3):
                lanes = slice((b - first) * 128, (b - first) * 128 + 128)
                c_ref[b, pl.ds(row, 16), :] = value[0:16, lanes] + sign * value[16:32, lanes]

    by_parts(group, body)

    @pl.when(group == 5)
    def _():
        lane = lax.broadcasted_iota(jnp.int32, (96, 128), 1)
        for c in range(8):
            block = jnp.concatenate(
                [c_ref[b, pl.ds(c, 96, stride=8), :] for b in range(3)], axis=1
            )
            block = jnp.concatenate([block, jnp.zeros((32, DEGREES), F32)], axis=0).T
            first = jnp.where(lane < 96, block[288:384], pltpu.roll(block[0:96], 96, 1))
            second = jnp.where(lane < 72, block[192:288], pltpu.roll(block[96:192], 72, 1))
            q_ref[0, pl.ds(c, 96, stride=8), :] = first
            q_ref[1, pl.ds(c, 96, stride=8), :] = second
        o_ref[...] = jnp.concatenate(
            [q_ref[0].reshape(32, 24, 128), q_ref[1].reshape(32, 24, 128)], axis=1
        ).astype(BF16)


def analyse(position, pieces, table):
    return call(
        analyse_kernel,
        jax.ShapeDtypeStruct((32, 48, 128), BF16),
        [position, *pieces, table, table, table],
        grid=(6,),
        scratch=[
            pltpu.VMEM((8, 768, 128), BF16),
            pltpu.VMEM((3, 768, 128), F32),
            pltpu.VMEM((2, 768, 128), F32),
        ],
        specs=[SMEM] + [None] * 8 + TABLE,
        us=10,
        name="analyse",
    )


def pair_rows(ref, p):
    return ref[:, p * 8 : p * 8 + 8, :].astype(F32).reshape(CH, 128).astype(BF16)


def mix_kernel(a_ref, w_ref, o_ref):
    lane = lax.broadcasted_iota(jnp.int32, (CH, 128), 1)
    pieces = []
    for p in range(6):
        half, e = divmod(p, 3)
        rows = pair_rows(a_ref, p)
        high = jnp.dot(w_ref[3 - half, :, e].reshape(CH, CH), rows, preferred_element_type=F32)
        low = jnp.dot(w_ref[half, :, e].reshape(CH, CH), rows, preferred_element_type=F32)
        pieces.append(jnp.where(lane < 96 - 24 * half, high, low).reshape(32, 8, 128))
    o_ref[...] = jnp.concatenate(pieces, axis=1).astype(BF16)


def mix(adjoint, mixing):
    return call(
        mix_kernel,
        jax.ShapeDtypeStruct((32, 48, 128), BF16),
        [adjoint, mixing],
        us=3,
        name="mix",
    )


PARTS = jax.ShapeDtypeStruct((4, 3, 128, CH), F32)


def grad_kernel(p_ref, c_ref, a_ref, near_ref, far_ref, s_ref):
    lane = lax.broadcasted_iota(jnp.int32, (CH, 128), 1)
    for p in range(6):
        half, e = divmod(p, 3)
        left, right = pair_rows(c_ref, p), pair_rows(a_ref, p)
        inside = lane < 96 - 24 * half
        zero = jnp.zeros_like(left)
        high = lax.dot_general(jnp.where(inside, left, zero), right, NT, preferred_element_type=F32)
        low = lax.dot_general(jnp.where(inside, zero, left), right, NT, preferred_element_type=F32)
        for n in range(2):
            s_ref[2 * (3 - half) + n, e] = high[n * 128 : n * 128 + 128]
            s_ref[2 * half + n, e] = low[n * 128 : n * 128 + 128]
    for dx in range(4):
        near_ref[dx] = s_ref[partner(p_ref[0], 2 * dx)[0]]
        far_ref[dx] = s_ref[partner(p_ref[0], 2 * dx + 1)[0]]


def weight_sums(position, coefficients, adjoint):
    return call(
        grad_kernel,
        (PARTS, PARTS),
        [position, coefficients, adjoint],
        scratch=[pltpu.VMEM((8, 3, 128, CH), F32)],
        specs=[SMEM, None, None],
        us=4,
        name="grad",
    )


def add_kernel(a_ref, b_ref, *o_refs):
    for dx in range(4):
        o_refs[dx][...] = a_ref[dx] + b_ref[dx]


def add_cores(near, far):
    piece = jax.ShapeDtypeStruct((3, 128, CH), F32)
    return call(add_kernel, (piece,) * 4, [near, far], us=3, name="add")


def total_kernel(y_ref, *refs):
    pieces, o_refs, s_ref = refs[:4], refs[4:8], refs[8]
    s_ref[...] = (pieces[0][...] + pieces[1][...]) + (pieces[2][...] + pieces[3][...])
    for step in range(4):
        row = pl.multiple_of((y_ref[0] + step) % 4 * 32, 32)
        o_refs[step][...] = s_ref[:, pl.ds(row, 32), :]


def total_sums(y, pieces):
    return call(
        total_kernel,
        (jax.ShapeDtypeStruct((3, 32, CH), F32),) * 4,
        [y, *pieces],
        scratch=[pltpu.VMEM((3, 128, CH), F32)],
        specs=[SMEM] + [None] * 4,
        us=3,
        name="total",
    )


def gather_kernel(p_ref, *refs):
    for k in range(8):
        refs[8][partner(p_ref[0], k)[1]] = refs[k][...]


def gather(position, pieces):
    return call(
        gather_kernel,
        jax.ShapeDtypeStruct((8, 3, 128, CH), BF16),
        [position, *pieces],
        specs=[SMEM] + [None] * 8,
        us=2,
        name="gather",
    )


def synthesise_kernel(p_ref, m_ref, w_ref, *refs):
    t_refs, o_refs, (q_ref, c_ref, b_ref) = refs[:3], refs[3:11], refs[11:]
    group = pl.program_id(0)
    position = p_ref[0]

    @pl.when(group == 0)
    def _():
        mixed = m_ref[...].astype(F32)
        q_ref[0] = mixed[:, 0:24, :].reshape(768, 128)
        q_ref[1] = mixed[:, 24:48, :].reshape(768, 128)
        for c in range(8):
            first = q_ref[0, pl.ds(c, 96, stride=8), :]
            second = q_ref[1, pl.ds(c, 96, stride=8), :]
            block = jnp.concatenate(
                [pltpu.roll(first, 32, 1), pltpu.roll(second, 56, 1), second, first], axis=0
            )
            block = block.T[0:96, :]
            for b in range(3):
                c_ref[b, pl.ds(c, 96, stride=8), :] = block[:, b * 128 : b * 128 + 128]

    sign = signs(position, 16)

    def body(first):
        for s in range(8):
            row = pl.multiple_of(group * 128 + s * 16, 16)
            north = [c_ref[b, pl.ds(row, 16), :] for b in range(first, 3)]
            south = [a * sign for a in north]
            left = jnp.concatenate(
                [jnp.concatenate(north, axis=1), jnp.concatenate(south, axis=1)], axis=0
            ).astype(BF16)
            right = jnp.concatenate([t_refs[b][0, s] for b in range(first, 3)], axis=0)
            value = jnp.dot(left, right, preferred_element_type=F32)
            for d in range(4):
                lanes = slice(d * 128, d * 128 + 128)
                mirror = slice((7 - d) * 128, (7 - d) * 128 + 128)
                b_ref[d, pl.ds(row, 16), :] = (value[0:16, lanes] * w_ref[0:1, lanes]).astype(BF16)
                b_ref[7 - d, pl.ds(row, 16), :] = (
                    value[16:32, lanes] * w_ref[0:1, mirror]
                ).astype(BF16)

    by_parts(group, body)

    @pl.when(group == 5)
    def _():
        for k in range(8):
            o_refs[k][...] = b_ref[partner(position, k)[0]]


def synthesise(position, mixed, table, weights):
    return call(
        synthesise_kernel,
        (PIECE,) * 8,
        [position, mixed, weights, table, table, table],
        grid=(6,),
        scratch=[
            pltpu.VMEM((2, 768, 128), F32),
            pltpu.VMEM((3, 768, 128), F32),
            pltpu.VMEM((8, 768, 128), BF16),
        ],
        specs=[SMEM, None, None] + TABLE,
        us=10,
        name="synthesise",
    )


def inverse_kernel(p_ref, *refs):
    pieces, (f_ref, o_ref, s_ref, t_ref) = refs[:8], refs[8:]
    position = p_ref[0]
    south = position >= 4
    for k in range(8):
        start = pl.multiple_of(partner(position, k)[1] * 768, 768)
        s_ref[pl.ds(start, 768), :] = pieces[k][...].astype(F32)
    low = lax.broadcasted_iota(jnp.int32, (11, 128), 1) < 64

    def one(pair, _):
        left = jnp.concatenate(
            [s_ref[pl.ds(2 * pair + b, 768, stride=8), :].astype(BF16) for b in range(2)], axis=1
        )
        grid = lax.dot_general(left, f_ref[...], TN, preferred_element_type=F32)
        for b in range(2):
            for zlo in range(4):
                place = jnp.where(south, 3 - zlo, zlo) * (8 * 264) + 2 * pair + b
                row = b * 128 + zlo * 32
                even, odd = grid[row : row + 11], grid[row + 16 : row + 27]
                for o in range(8):
                    base = place + o * 264
                    lanes = slice(o * 128, o * 128 + 128)
                    t_ref[pl.ds(base, 11, stride=8), :] = even[:, lanes]
                    t_ref[pl.ds(base + 88, 11, stride=8), :] = odd[:, lanes]
                    lanes = slice(1024 + o // 2 * 128, 1152 + o // 2 * 128)
                    first, last = even[:, lanes], odd[:, lanes]
                    if o % 2 == 0:
                        tail = jnp.where(low, first, pltpu.roll(last, 64, 1))
                    else:
                        tail = jnp.where(low, pltpu.roll(first, 64, 1), last)
                    t_ref[pl.ds(base + 176, 11, stride=8), :] = tail
        return 0

    lax.fori_loop(0, 4, one, 0)
    o_ref[...] = t_ref[...].reshape(32, 264, 128).astype(BF16)


def inverse(position, pieces, table):
    return call(
        inverse_kernel,
        jax.ShapeDtypeStruct((32, 264, 128), BF16),
        [position, *pieces, table],
        scratch=[pltpu.VMEM((6144, 128), F32), pltpu.VMEM((32 * 264, 128), F32)],
        specs=[SMEM] + [None] * 9,
        us=9,
        name="inverse",
    )


def finish_kernel(p_ref, r_ref, g_ref, o_ref, s_ref):
    south = p_ref[0] >= 4
    s_ref[...] = r_ref[...].astype(F32)
    for pair in range(11):
        row = 176 + pair * 8
        tail = s_ref[:, row : row + 8, :].reshape(CH, 128).T
        for parity in range(2):
            j = 2 * pair + parity
            j = jnp.where(south, 21 - j, j)
            row = (parity * 11 + pair) * 8
            head = s_ref[:, row : row + 8, :].reshape(CH, 128).T
            o_ref[j, 0:128, :] = (g_ref[j, 0:128, :].astype(F32) + head).astype(BF16)
            rest = tail[parity * 64 : parity * 64 + 52]
            o_ref[j, 128:180, :] = (g_ref[j, 128:180, :].astype(F32) + rest).astype(BF16)


def finish(position, received, cotangent):
    return call(
        finish_kernel,
        jax.ShapeDtypeStruct((ROWS, POINTS, CH), BF16),
        [position, received, cotangent],
        scratch=[pltpu.VMEM((32, 264, 128), F32)],
        specs=[SMEM, None, None],
        us=4,
        name="finish",
    )


def swap(value):
    return lax.all_to_all(value, RING, split_axis=0, concat_axis=0, tiled=True)


def cross(pieces):
    moved = [pieces[0]]
    for k in range(1, 8):
        pairs = [(p, partner(p, k)[0]) for p in range(8)]
        moved.append(lax.ppermute(pieces[k], CROSS, pairs))
    return moved


def along_x(pieces):
    return [pieces[0]] + [
        lax.ppermute(pieces[dx], "x", [(i, (i + dx) % 4) for i in range(4)]) for dx in range(1, 4)
    ]


def other_core(value):
    return lax.ppermute(value, "core", [(0, 1), (1, 0)])


def turned(pieces):
    moved = []
    for step, piece in enumerate(pieces):
        pairs = [
            (core * 8 + zhi * 4 + y, zhi * 8 + core * 4 + (y + step) % 4)
            for core in range(2)
            for zhi in range(2)
            for y in range(4)
        ]
        moved.append(lax.ppermute(piece, ("core", "zhi", "y"), pairs))
    return moved


def in_order(pieces):
    y = lax.axis_index("y")
    out = jnp.zeros((4, *pieces[0].shape), pieces[0].dtype)
    for step, piece in enumerate(pieces):
        out = lax.dynamic_update_index_in_dim(out, piece, (y + 4 - step) % 4, 0)
    return out


def after(value, *others):
    return lax.optimization_barrier((value, *others))[0]


def slot_rows():
    slot = jnp.arange(512, dtype=jnp.int32)
    device, within = slot // 128, slot % 128
    zlo, parity, pair = within // 32, within % 32 // 16, within % 16
    row = (device // 2) * 176 + zlo * 44 + (device % 2) * 22 + 2 * pair + parity
    mirrored = (NLAT - 1 - row).reshape(4, 128)[::-1].reshape(512)
    valid = pair < 11
    return jnp.concatenate([row, mirrored]), jnp.concatenate([valid, valid])


def local(grid_input, cotangent, mixing):
    position = lax.axis_index("x") * 2 + lax.axis_index("core")
    y = lax.axis_index("y")
    where = jnp.full((1,), position, jnp.int32)
    packed_g = pack(where, cotangent)
    sent_g = swap(packed_g)
    packed_x = pack(where, after(grid_input, packed_g))
    mixing = after(mixing, packed_g)
    weights = in_order(
        turned([lax.dynamic_slice_in_dim(mixing, (y + step) % 4 * 3, 3, 0) for step in range(4)])
    )
    weights = jnp.transpose(weights, (1, 0, 2, 3)).reshape(3, 128, CH)
    row, valid = slot_rows()
    colatitude = (row.astype(F32) + 0.5) * (math.pi / NLAT)
    sine = jnp.sin(colatitude)
    quadrature = jnp.where(valid, math.pi / NLAT * sine, 0.0)
    cosine = jnp.where(valid, jnp.cos(colatitude), 0.0)[0:512]
    orders = 8 * jnp.arange(48, dtype=jnp.int32) + position
    order_value = orders.astype(F32)[:, None]
    counter = jnp.arange(1, ORDERS + 1, dtype=F32)[None, :]
    log_terms = jnp.where(counter <= order_value, jnp.log1p(0.5 / counter), 0.0)
    logs = (
        0.5 * math.log(0.5)
        + 0.5 * jnp.sum(log_terms, axis=1, keepdims=True)
        + order_value * jnp.log(sine[0:512])[None, :]
    )
    logs = jnp.where(valid[None, 0:512], logs, -1e30)
    table = legendre_table(
        after(jnp.broadcast_to(order_value, (48, 128)), packed_x),
        jnp.broadcast_to(cosine[None, :], (8, 512)),
        logs,
    )
    forward, backward = fourier_tables()
    own = lax.dynamic_slice_in_dim(quadrature, position * 128, 128)
    sent_g = after(sent_g, packed_x, forward, backward, table, weights)
    sent_x = swap(after(packed_x, sent_g))
    pieces_g = fourier(where, sent_g, backward, jnp.ones((8, 128), F32))
    packed_adjoint = analyse(where, cross(pieces_g), table)
    adjoint = swap(after(packed_adjoint, sent_x))
    weights = along_x([after(weights, packed_adjoint, sent_x)] * 4)
    weights = [w for near in weights for w in (near, other_core(near))]
    weights = gather(where, weights).reshape(4, 2, 3, 128, CH)
    pieces_x = fourier(where, sent_x, forward, jnp.broadcast_to(own[None, :], (8, 128)))
    mixed = swap(mix(after(adjoint, pieces_x[0]), weights))
    coefficients = analyse(where, cross(pieces_x), table)
    mixed = after(mixed, coefficients)
    back = synthesise(where, mixed, table, jnp.broadcast_to(quadrature[None, :], (8, 1024)))
    coefficients = swap(after(coefficients, back[0]))
    packed_back = inverse(where, cross(back), forward)
    grid_back = swap(packed_back)
    near, far = weight_sums(where, after(coefficients, packed_back), adjoint)
    total = along_x(add_cores(near, other_core(far)))
    total = turned(total_sums(jnp.full((1,), y, jnp.int32), total))
    input_grad = finish(where, grid_back, cotangent)
    total[0] = after(total[0], input_grad)
    return input_grad, in_order(total).reshape(12, 32, CH)


def solution(mesh):
    fine = Mesh(mesh.devices.reshape(4, 4, 2, 2, 4), ("x", "zlo", "core", "zhi", "y"))
    spec = P(("x", "zlo", "core"), ("zhi", "y"), None)
    return jax.shard_map(
        local, mesh=fine, in_specs=(spec, spec, spec), out_specs=(spec, spec), check_vma=False
    )
```

```python
import math

import jax
import jax.numpy as jnp
from jax import lax
from jax.experimental import pallas as pl
from jax.experimental.pallas import tpu as pltpu
from jax.sharding import Mesh, PartitionSpec as P

F32 = jnp.float32
BF16 = jnp.bfloat16
NLON, NLAT, ORDERS, DEGREES = 1440, 704, 384, 384
ROWS, POINTS, CH = 22, 180, 256
RING = ("zlo", "zhi", "y")
CROSS = ("x", "core")
NT = (((1,), (1,)), ((), ()))
TN = (((0,), (0,)), ((), ()))
SMEM = pl.BlockSpec(memory_space=pltpu.SMEM)
PIECE = jax.ShapeDtypeStruct((768, 128), BF16)


def call(body, outs, ins, grid=(1,), scratch=(), us=1, specs=None, out_specs=None, name=None):
    whole = lambda a: pl.BlockSpec(a.shape, lambda *_, n=len(a.shape): (0,) * n)
    specs = specs or [None] * len(ins)
    return pl.pallas_call(
        body,
        out_shape=outs,
        grid=grid,
        in_specs=[whole(a) if s is None else s for a, s in zip(ins, specs)],
        out_specs=out_specs or jax.tree.map(whole, outs),
        scratch_shapes=list(scratch),
        compiler_params=pltpu.CompilerParams(vmem_limit_bytes=56 * 2**20),
        cost_estimate=pl.CostEstimate(
            flops=us * 1_100_000_000, bytes_accessed=us * 1_000_000, transcendentals=0
        ),
        name=name,
    )(*ins)


def partner(position, k):
    dx, dc = divmod(k, 2)
    x, core = position // 2, position % 2
    core = (core + dc) % 2
    return ((x + dx) % 4) * 2 + core, ((x + 4 - dx) % 4) * 2 + core


def pack_kernel(p_ref, x_ref, o_ref, s_ref):
    south = p_ref[0] >= 4
    eye = (
        lax.broadcasted_iota(jnp.int32, (CH, CH), 0) == lax.broadcasted_iota(jnp.int32, (CH, CH), 1)
    ).astype(BF16)
    zeros = jnp.zeros((CH, 76), F32)
    for pair in range(11):
        tail = None
        for parity in range(2):
            j = 2 * pair + parity
            j = jnp.where(south, 21 - j, j)
            head = lax.dot_general(eye, x_ref[j, 0:128, :], NT, preferred_element_type=F32)
            row = (parity * 11 + pair) * 8
            s_ref[:, row : row + 8, :] = head.reshape(32, 8, 128)
            rest = lax.dot_general(eye, x_ref[j, 128:180, :], NT, preferred_element_type=F32)
            rest = jnp.concatenate([rest, zeros], axis=1)
            tail = rest if parity == 0 else tail + pltpu.roll(rest, 64, 1)
        row = 176 + pair * 8
        s_ref[:, row : row + 8, :] = tail.reshape(32, 8, 128)
    o_ref[...] = s_ref[...].astype(BF16)


def pack(position, x):
    return call(
        pack_kernel,
        jax.ShapeDtypeStruct((32, 264, 128), BF16),
        [position, x],
        scratch=[pltpu.VMEM((32, 264, 128), F32)],
        specs=[SMEM, None],
        us=5,
        name="pack",
    )


def waves_kernel(c_ref, s_ref, f_ref, b_ref):
    for d in range(8):
        rows = slice(d * 96, d * 96 + 96)
        order = 8 * (lax.broadcasted_iota(jnp.int32, (96, 128), 0) // 2) + d
        factor = jnp.where(order == 0, 1.0 / NLON, 2.0 / NLON)
        low = lax.broadcasted_iota(jnp.int32, (96, 128), 1) < 64

        def turned(o, lanes):
            angle = (d * o) % 8 * math.pi / 4
            return c_ref[rows, lanes] * math.cos(angle) - s_ref[rows, lanes] * math.sin(angle)

        def put(value, place):
            f_ref[rows, place * 128 : place * 128 + 128] = value.astype(BF16)
            b_ref[rows, place * 128 : place * 128 + 128] = (value * factor).astype(BF16)

        for o in range(8):
            put(turned(o, slice(0, 128)), o)
        for o in range(4):
            tails = [turned(2 * o + i, slice(128, 256)) for i in range(2)]
            put(jnp.where(low, tails[0], tails[1]), 8 + o)


def fourier_tables():
    q = jnp.arange(768, dtype=jnp.int32)
    order, quarter = 8 * (q % 96 // 2) + q // 96, q % 2
    lane = jnp.arange(256, dtype=jnp.int32)
    point = jnp.where(lane < 128, lane, 128 + lane % 64)
    valid = (point < POINTS)[None, :]
    phase = (point[None, :] * order[:, None] + 360 * quarter[:, None]) % NLON
    angle = phase.astype(F32) * (2.0 * math.pi / NLON)
    table = jax.ShapeDtypeStruct((768, 1536), BF16)
    return call(
        waves_kernel,
        (table, table),
        [jnp.where(valid, jnp.cos(angle), 0.0), jnp.where(valid, jnp.sin(angle), 0.0)],
        us=4,
        name="waves",
    )


def fourier_kernel(p_ref, r_ref, f_ref, w_ref, *refs):
    o_refs, (s_ref, k_ref, t_ref) = refs[:8], refs[8:]
    position = p_ref[0]
    south = position >= 4
    s_ref[0 : 32 * 264, :] = r_ref[...].reshape(32 * 264, 128).astype(F32)
    s_ref[32 * 264 :, :] = jnp.zeros((64, 128), F32)
    low = lax.broadcasted_iota(jnp.int32, (16, 128), 1) < 64

    def one(pair, _):
        for b in range(2):
            c = 2 * pair + b
            for zlo in range(4):
                source = jnp.where(south, 3 - zlo, zlo) * (8 * 264) + c
                row = b * 128 + zlo * 32
                tails = []
                for o in range(8):
                    base = source + o * 264
                    for parity in range(2):
                        k_ref[row + parity * 16 : row + parity * 16 + 16, o * 128 : o * 128 + 128] = (
                            s_ref[pl.ds(base + parity * 88, 16, stride=8), :].astype(BF16)
                        )
                    tails.append(s_ref[pl.ds(base + 176, 16, stride=8), :])
                for o in range(4):
                    even, odd = tails[2 * o], tails[2 * o + 1]
                    lanes = slice(1024 + o * 128, 1152 + o * 128)
                    north = jnp.where(low, even, pltpu.roll(odd, 64, 1))
                    k_ref[row : row + 16, lanes] = north.astype(BF16)
                    other = jnp.where(low, pltpu.roll(even, 64, 1), odd)
                    k_ref[row + 16 : row + 32, lanes] = other.astype(BF16)
        spec = lax.dot_general(f_ref[...], k_ref[...], NT, preferred_element_type=F32)
        for b in range(2):
            value = spec[:, b * 128 : b * 128 + 128] * w_ref[0:1, :]
            t_ref[pl.ds(2 * pair + b, 768, stride=8), :] = value
        return 0

    lax.fori_loop(0, 4, one, 0)
    for k in range(8):
        start = pl.multiple_of(partner(position, k)[0] * 768, 768)
        o_refs[k][...] = t_ref[pl.ds(start, 768), :].astype(BF16)


def fourier(position, received, table, weights, us):
    return call(
        fourier_kernel,
        (PIECE,) * 8,
        [position, received, table, weights],
        scratch=[
            pltpu.VMEM((32 * 264 + 64, 128), F32),
            pltpu.VMEM((256, 1536), BF16),
            pltpu.VMEM((6144, 128), F32),
        ],
        specs=[SMEM, None, None, None],
        us=us,
        name="fourier",
    )


def block_orders(i):
    return jnp.where(i < 6, i // 3, jnp.where(i < 10, 2 + (i - 6) // 2, i - 6))


def block_degrees(i):
    return jnp.where(i < 6, i % 3, jnp.where(i < 10, 1 + i % 2, 2))


def table_kernel(m_ref, cos_ref, log_ref, o_ref, s_ref, v_ref):
    i = pl.program_id(0)
    group, part = block_orders(i), block_degrees(i)

    @pl.when(part == group // 2)
    def _():
        v_ref[0] = jnp.zeros((8, 512), F32)
        v_ref[1] = jnp.zeros((8, 512), F32)
        v_ref[2] = log_ref[...]

    order = m_ref[...]
    square = order * order
    cosine = cos_ref[...]
    wide = lambda a: jnp.concatenate([a] * 4, axis=1)

    def steps(n, carried):
        previous, earlier, scale = carried
        size = jnp.exp(scale)
        first = jnp.full((8, 128), part * 128 + n * 8, jnp.int32).astype(F32)

        def ratios(degree):
            above = jnp.maximum(4.0 * degree * degree - 1.0, 0.0)
            below = jnp.maximum(degree * degree - square, 0.0)
            root = lax.rsqrt(jnp.maximum(above * below, 1e-6))
            return above * root, below * root

        _, shrink = ratios(jnp.maximum(first - 1.0, 0.0))
        for u in range(8):
            l = n * 8 + u
            degree = first + float(u)
            growth, inverse_growth = ratios(degree)
            current = wide(growth) * (cosine * previous) - wide(growth * shrink) * earlier
            shrink = inverse_growth
            current = jnp.where(wide(degree == order), 1.0, current)
            value = current * size
            for d in range(4):
                s_ref[d, pl.ds(pl.multiple_of(l * 8, 8), 8), :] = value[:, d * 128 : d * 128 + 128]
            previous, earlier = current, previous
        over = jnp.maximum(jnp.abs(previous), jnp.abs(earlier)) > 1e5
        factor = jnp.where(over, 1e-10, 1.0)
        scale = scale + jnp.where(over, math.log(1e10), 0.0)
        return previous * factor, earlier * factor, scale

    state = lax.fori_loop(0, 16, steps, (v_ref[0], v_ref[1], v_ref[2]))
    for n in range(3):
        v_ref[n] = state[n]
    for s in range(8):
        for d in range(4):
            o_ref[0, s, :, d * 128 : d * 128 + 128] = s_ref[
                d, pl.ds(s, 128, stride=8), :
            ].astype(BF16)


def legendre_table(orders, cosine, logs):
    return call(
        table_kernel,
        jax.ShapeDtypeStruct((12, 8, 128, 512), BF16),
        [orders, cosine, logs],
        grid=(12,),
        scratch=[pltpu.VMEM((4, 1024, 128), F32), pltpu.VMEM((3, 8, 512), F32)],
        specs=[
            pl.BlockSpec((8, 128), lambda i: (block_orders(i), 0)),
            None,
            pl.BlockSpec((8, 512), lambda i: (block_orders(i), 0)),
        ],
        out_specs=pl.BlockSpec((1, 8, 128, 512), lambda i: (i, 0, 0, 0)),
        us=25,
        name="legendre",
    )


def pick(g, *values):
    out = values[-1]
    for n in reversed(range(len(values) - 1)):
        out = jnp.where(g == n, values[n], out)
    return out


TABLE = [
    pl.BlockSpec((1, 8, 128, 512), lambda g, v=v: (pick(g, *v), 0, 0, 0))
    for v in ((0, 3), (1, 4, 6, 8), (2, 5, 7, 9, 10, 11))
]


def by_parts(group, body):
    for first in range(3):

        @pl.when(group // 2 == first)
        def _(first=first):
            body(first)


def signs(position, rows):
    lane = lax.broadcasted_iota(jnp.int32, (rows, 128), 1)
    return jnp.where((lane + position) % 2 == 0, 1.0, -1.0)


def analyse_kernel(p_ref, *refs):
    pieces, t_refs, (o_ref, s_ref, c_ref, q_ref) = refs[:8], refs[8:11], refs[11:]
    group = pl.program_id(0)
    position = p_ref[0]

    @pl.when(group == 0)
    def _():
        for k in range(8):
            s_ref[partner(position, k)[1]] = pieces[k][...]
        c_ref[...] = jnp.zeros_like(c_ref)

    sign = signs(position, 16)

    def body(first):
        for s in range(8):
            row = pl.multiple_of(group * 128 + s * 16, 16)
            north = jnp.concatenate([s_ref[d, pl.ds(row, 16), :] for d in range(4)], axis=1)
            south = jnp.concatenate([s_ref[7 - d, pl.ds(row, 16), :] for d in range(4)], axis=1)
            value = lax.dot_general(
                jnp.concatenate([north, south], axis=0),
                jnp.concatenate([t_refs[b][0, s] for b in range(first, 3)], axis=0),
                NT,
                preferred_element_type=F32,
            )
            for b in range(first, 3):
                lanes = slice((b - first) * 128, (b - first) * 128 + 128)
                c_ref[b, pl.ds(row, 16), :] = value[0:16, lanes] + sign * value[16:32, lanes]

    by_parts(group, body)

    @pl.when(group == 5)
    def _():
        lane = lax.broadcasted_iota(jnp.int32, (96, 128), 1)
        for c in range(8):
            block = jnp.concatenate(
                [c_ref[b, pl.ds(c, 96, stride=8), :] for b in range(3)], axis=1
            )
            block = jnp.concatenate([block, jnp.zeros((32, DEGREES), F32)], axis=0).T
            first = jnp.where(lane < 96, block[288:384], pltpu.roll(block[0:96], 96, 1))
            second = jnp.where(lane < 72, block[192:288], pltpu.roll(block[96:192], 72, 1))
            q_ref[0, pl.ds(c, 96, stride=8), :] = first
            q_ref[1, pl.ds(c, 96, stride=8), :] = second
        o_ref[...] = jnp.concatenate(
            [q_ref[0].reshape(32, 24, 128), q_ref[1].reshape(32, 24, 128)], axis=1
        ).astype(BF16)


def analyse(position, pieces, table):
    return call(
        analyse_kernel,
        jax.ShapeDtypeStruct((32, 48, 128), BF16),
        [position, *pieces, table, table, table],
        grid=(6,),
        scratch=[
            pltpu.VMEM((8, 768, 128), BF16),
            pltpu.VMEM((3, 768, 128), F32),
            pltpu.VMEM((2, 768, 128), F32),
        ],
        specs=[SMEM] + [None] * 8 + TABLE,
        us=10,
        name="analyse",
    )


def pair_rows(ref, p):
    return ref[:, p * 8 : p * 8 + 8, :].astype(F32).reshape(CH, 128).astype(BF16)


def mix_kernel(a_ref, w_ref, o_ref):
    lane = lax.broadcasted_iota(jnp.int32, (CH, 128), 1)
    pieces = []
    for p in range(6):
        half, e = divmod(p, 3)
        rows = pair_rows(a_ref, p)
        high = jnp.dot(w_ref[3 - half, :, e].reshape(CH, CH), rows, preferred_element_type=F32)
        low = jnp.dot(w_ref[half, :, e].reshape(CH, CH), rows, preferred_element_type=F32)
        pieces.append(jnp.where(lane < 96 - 24 * half, high, low).reshape(32, 8, 128))
    o_ref[...] = jnp.concatenate(pieces, axis=1).astype(BF16)


def mix(adjoint, mixing):
    return call(
        mix_kernel,
        jax.ShapeDtypeStruct((32, 48, 128), BF16),
        [adjoint, mixing],
        us=3,
        name="mix",
    )


PARTS = jax.ShapeDtypeStruct((4, 3, 128, CH), F32)


def grad_kernel(p_ref, c_ref, a_ref, near_ref, far_ref, s_ref):
    lane = lax.broadcasted_iota(jnp.int32, (CH, 128), 1)
    for p in range(6):
        half, e = divmod(p, 3)
        left, right = pair_rows(c_ref, p), pair_rows(a_ref, p)
        inside = lane < 96 - 24 * half
        zero = jnp.zeros_like(left)
        high = lax.dot_general(jnp.where(inside, left, zero), right, NT, preferred_element_type=F32)
        low = lax.dot_general(jnp.where(inside, zero, left), right, NT, preferred_element_type=F32)
        for n in range(2):
            s_ref[2 * (3 - half) + n, e] = high[n * 128 : n * 128 + 128]
            s_ref[2 * half + n, e] = low[n * 128 : n * 128 + 128]
    for dx in range(4):
        near_ref[dx] = s_ref[partner(p_ref[0], 2 * dx)[0]]
        far_ref[dx] = s_ref[partner(p_ref[0], 2 * dx + 1)[0]]


def weight_sums(position, coefficients, adjoint):
    return call(
        grad_kernel,
        (PARTS, PARTS),
        [position, coefficients, adjoint],
        scratch=[pltpu.VMEM((8, 3, 128, CH), F32)],
        specs=[SMEM, None, None],
        us=4,
        name="grad",
    )


def add_kernel(a_ref, b_ref, *o_refs):
    for dx in range(4):
        o_refs[dx][...] = a_ref[dx] + b_ref[dx]


def add_cores(near, far):
    piece = jax.ShapeDtypeStruct((3, 128, CH), F32)
    return call(add_kernel, (piece,) * 4, [near, far], us=3, name="add")


def total_kernel(y_ref, *refs):
    pieces, o_refs, s_ref = refs[:4], refs[4:8], refs[8]
    s_ref[...] = (pieces[0][...] + pieces[1][...]) + (pieces[2][...] + pieces[3][...])
    for step in range(4):
        row = pl.multiple_of((y_ref[0] + step) % 4 * 32, 32)
        o_refs[step][...] = s_ref[:, pl.ds(row, 32), :]


def total_sums(y, pieces):
    return call(
        total_kernel,
        (jax.ShapeDtypeStruct((3, 32, CH), F32),) * 4,
        [y, *pieces],
        scratch=[pltpu.VMEM((3, 128, CH), F32)],
        specs=[SMEM] + [None] * 4,
        us=3,
        name="total",
    )


def gather_kernel(p_ref, *refs):
    for k in range(8):
        refs[8][partner(p_ref[0], k)[1]] = refs[k][...]


def gather(position, pieces):
    return call(
        gather_kernel,
        jax.ShapeDtypeStruct((8, 3, 128, CH), BF16),
        [position, *pieces],
        specs=[SMEM] + [None] * 8,
        us=1,
        name="gather",
    )


def synthesise_kernel(p_ref, m_ref, w_ref, *refs):
    t_refs, o_refs, (q_ref, c_ref, b_ref) = refs[:3], refs[3:11], refs[11:]
    group = pl.program_id(0)
    position = p_ref[0]

    @pl.when(group == 0)
    def _():
        mixed = m_ref[...].astype(F32)
        q_ref[0] = mixed[:, 0:24, :].reshape(768, 128)
        q_ref[1] = mixed[:, 24:48, :].reshape(768, 128)
        for c in range(8):
            first = q_ref[0, pl.ds(c, 96, stride=8), :]
            second = q_ref[1, pl.ds(c, 96, stride=8), :]
            block = jnp.concatenate(
                [pltpu.roll(first, 32, 1), pltpu.roll(second, 56, 1), second, first], axis=0
            )
            block = block.T[0:96, :]
            for b in range(3):
                c_ref[b, pl.ds(c, 96, stride=8), :] = block[:, b * 128 : b * 128 + 128]

    sign = signs(position, 16)

    def body(first):
        for s in range(8):
            row = pl.multiple_of(group * 128 + s * 16, 16)
            north = [c_ref[b, pl.ds(row, 16), :] for b in range(first, 3)]
            south = [a * sign for a in north]
            left = jnp.concatenate(
                [jnp.concatenate(north, axis=1), jnp.concatenate(south, axis=1)], axis=0
            ).astype(BF16)
            right = jnp.concatenate([t_refs[b][0, s] for b in range(first, 3)], axis=0)
            value = jnp.dot(left, right, preferred_element_type=F32)
            for d in range(4):
                lanes = slice(d * 128, d * 128 + 128)
                mirror = slice((7 - d) * 128, (7 - d) * 128 + 128)
                b_ref[d, pl.ds(row, 16), :] = (value[0:16, lanes] * w_ref[0:1, lanes]).astype(BF16)
                b_ref[7 - d, pl.ds(row, 16), :] = (
                    value[16:32, lanes] * w_ref[0:1, mirror]
                ).astype(BF16)

    by_parts(group, body)

    @pl.when(group == 5)
    def _():
        for k in range(8):
            o_refs[k][...] = b_ref[partner(position, k)[0]]


def synthesise(position, mixed, table, weights):
    return call(
        synthesise_kernel,
        (PIECE,) * 8,
        [position, mixed, weights, table, table, table],
        grid=(6,),
        scratch=[
            pltpu.VMEM((2, 768, 128), F32),
            pltpu.VMEM((3, 768, 128), F32),
            pltpu.VMEM((8, 768, 128), BF16),
        ],
        specs=[SMEM, None, None] + TABLE,
        us=10,
        name="synthesise",
    )


def inverse_kernel(p_ref, *refs):
    pieces, (f_ref, o_ref, s_ref, t_ref) = refs[:8], refs[8:]
    position = p_ref[0]
    south = position >= 4
    for k in range(8):
        start = pl.multiple_of(partner(position, k)[1] * 768, 768)
        s_ref[pl.ds(start, 768), :] = pieces[k][...].astype(F32)
    low = lax.broadcasted_iota(jnp.int32, (11, 128), 1) < 64

    def one(pair, _):
        left = jnp.concatenate(
            [s_ref[pl.ds(2 * pair + b, 768, stride=8), :].astype(BF16) for b in range(2)], axis=1
        )
        grid = lax.dot_general(left, f_ref[...], TN, preferred_element_type=F32)
        for b in range(2):
            for zlo in range(4):
                place = jnp.where(south, 3 - zlo, zlo) * (8 * 264) + 2 * pair + b
                row = b * 128 + zlo * 32
                even, odd = grid[row : row + 11], grid[row + 16 : row + 27]
                for o in range(8):
                    base = place + o * 264
                    lanes = slice(o * 128, o * 128 + 128)
                    t_ref[pl.ds(base, 11, stride=8), :] = even[:, lanes]
                    t_ref[pl.ds(base + 88, 11, stride=8), :] = odd[:, lanes]
                    lanes = slice(1024 + o // 2 * 128, 1152 + o // 2 * 128)
                    first, last = even[:, lanes], odd[:, lanes]
                    if o % 2 == 0:
                        tail = jnp.where(low, first, pltpu.roll(last, 64, 1))
                    else:
                        tail = jnp.where(low, pltpu.roll(first, 64, 1), last)
                    t_ref[pl.ds(base + 176, 11, stride=8), :] = tail
        return 0

    lax.fori_loop(0, 4, one, 0)
    o_ref[...] = t_ref[...].reshape(32, 264, 128).astype(BF16)


def inverse(position, pieces, table):
    return call(
        inverse_kernel,
        jax.ShapeDtypeStruct((32, 264, 128), BF16),
        [position, *pieces, table],
        scratch=[pltpu.VMEM((6144, 128), F32), pltpu.VMEM((32 * 264, 128), F32)],
        specs=[SMEM] + [None] * 9,
        us=9,
        name="inverse",
    )


def finish_kernel(p_ref, r_ref, g_ref, o_ref, s_ref):
    south = p_ref[0] >= 4
    s_ref[...] = r_ref[...].astype(F32)
    for pair in range(11):
        row = 176 + pair * 8
        tail = s_ref[:, row : row + 8, :].reshape(CH, 128).T
        for parity in range(2):
            j = 2 * pair + parity
            j = jnp.where(south, 21 - j, j)
            row = (parity * 11 + pair) * 8
            head = s_ref[:, row : row + 8, :].reshape(CH, 128).T
            o_ref[j, 0:128, :] = (g_ref[j, 0:128, :].astype(F32) + head).astype(BF16)
            rest = tail[parity * 64 : parity * 64 + 52]
            o_ref[j, 128:180, :] = (g_ref[j, 128:180, :].astype(F32) + rest).astype(BF16)


def finish(position, received, cotangent):
    return call(
        finish_kernel,
        jax.ShapeDtypeStruct((ROWS, POINTS, CH), BF16),
        [position, received, cotangent],
        scratch=[pltpu.VMEM((32, 264, 128), F32)],
        specs=[SMEM, None, None],
        us=4,
        name="finish",
    )


def swap(value):
    return lax.all_to_all(value, RING, split_axis=0, concat_axis=0, tiled=True)


def cross(pieces):
    moved = [pieces[0]]
    for k in range(1, 8):
        pairs = [(p, partner(p, k)[0]) for p in range(8)]
        moved.append(lax.ppermute(pieces[k], CROSS, pairs))
    return moved


def along_x(pieces):
    return [pieces[0]] + [
        lax.ppermute(pieces[dx], "x", [(i, (i + dx) % 4) for i in range(4)]) for dx in range(1, 4)
    ]


def other_core(value):
    return lax.ppermute(value, "core", [(0, 1), (1, 0)])


def turned(pieces):
    moved = []
    for step, piece in enumerate(pieces):
        pairs = [
            (core * 8 + zhi * 4 + y, zhi * 8 + core * 4 + (y + step) % 4)
            for core in range(2)
            for zhi in range(2)
            for y in range(4)
        ]
        moved.append(lax.ppermute(piece, ("core", "zhi", "y"), pairs))
    return moved


def in_order(pieces):
    y = lax.axis_index("y")
    out = jnp.zeros((4, *pieces[0].shape), pieces[0].dtype)
    for step, piece in enumerate(pieces):
        out = lax.dynamic_update_index_in_dim(out, piece, (y + 4 - step) % 4, 0)
    return out


def after(value, *others):
    return lax.optimization_barrier((value, *others))[0]


def slot_rows():
    slot = jnp.arange(512, dtype=jnp.int32)
    device, within = slot // 128, slot % 128
    zlo, parity, pair = within // 32, within % 32 // 16, within % 16
    row = (device // 2) * 176 + zlo * 44 + (device % 2) * 22 + 2 * pair + parity
    mirrored = (NLAT - 1 - row).reshape(4, 128)[::-1].reshape(512)
    valid = pair < 11
    return jnp.concatenate([row, mirrored]), jnp.concatenate([valid, valid])


def local(grid_input, cotangent, mixing):
    position = lax.axis_index("x") * 2 + lax.axis_index("core")
    y = lax.axis_index("y")
    where = jnp.full((1,), position, jnp.int32)
    packed_g = pack(where, cotangent)
    sent_g = swap(packed_g)
    packed_x = pack(where, after(grid_input, packed_g))
    mixing = after(mixing, packed_g)
    weights = in_order(
        turned([lax.dynamic_slice_in_dim(mixing, (y + step) % 4 * 3, 3, 0) for step in range(4)])
    )
    weights = jnp.transpose(weights, (1, 0, 2, 3)).reshape(3, 128, CH)
    row, valid = slot_rows()
    colatitude = (row.astype(F32) + 0.5) * (math.pi / NLAT)
    sine = jnp.sin(colatitude)
    quadrature = jnp.where(valid, math.pi / NLAT * sine, 0.0)
    cosine = jnp.where(valid, jnp.cos(colatitude), 0.0)[0:512]
    orders = 8 * jnp.arange(48, dtype=jnp.int32) + position
    order_value = orders.astype(F32)[:, None]
    counter = jnp.arange(1, ORDERS + 1, dtype=F32)[None, :]
    log_terms = jnp.where(counter <= order_value, jnp.log1p(0.5 / counter), 0.0)
    logs = (
        0.5 * math.log(0.5)
        + 0.5 * jnp.sum(log_terms, axis=1, keepdims=True)
        + order_value * jnp.log(sine[0:512])[None, :]
    )
    logs = jnp.where(valid[None, 0:512], logs, -1e30)
    table = legendre_table(
        after(jnp.broadcast_to(order_value, (48, 128)), packed_x),
        jnp.broadcast_to(cosine[None, :], (8, 512)),
        logs,
    )
    forward, backward = fourier_tables()
    own = lax.dynamic_slice_in_dim(quadrature, position * 128, 128)
    sent_g = after(sent_g, packed_x, forward, backward, table, weights)
    sent_x = swap(after(packed_x, sent_g))
    pieces_g = fourier(where, sent_g, backward, jnp.ones((8, 128), F32), 9)
    packed_adjoint = analyse(where, cross(pieces_g), table)
    adjoint = swap(after(packed_adjoint, sent_x))
    weights = along_x([after(weights, packed_adjoint, sent_x)] * 4)
    weights = [w for near in weights for w in (near, other_core(near))]
    weights = gather(where, weights).reshape(4, 2, 3, 128, CH)
    pieces_x = fourier(where, sent_x, forward, jnp.broadcast_to(own[None, :], (8, 128)), 1)
    mixed = swap(mix(after(adjoint, pieces_x[0]), weights))
    coefficients = analyse(where, cross(pieces_x), table)
    mixed = after(mixed, coefficients)
    back = synthesise(where, mixed, table, jnp.broadcast_to(quadrature[None, :], (8, 1024)))
    coefficients = swap(after(coefficients, back[0]))
    packed_back = inverse(where, cross(back), forward)
    grid_back = swap(packed_back)
    near, far = weight_sums(where, after(coefficients, packed_back), adjoint)
    total = along_x(add_cores(near, other_core(far)))
    total = turned(total_sums(jnp.full((1,), y, jnp.int32), total))
    input_grad = finish(where, grid_back, cotangent)
    total[0] = after(total[0], input_grad)
    return input_grad, in_order(total).reshape(12, 32, CH)


def solution(mesh):
    fine = Mesh(mesh.devices.reshape(4, 4, 2, 2, 4), ("x", "zlo", "core", "zhi", "y"))
    spec = P(("x", "zlo", "core"), ("zhi", "y"), None)
    return jax.shard_map(
        local, mesh=fine, in_specs=(spec, spec, spec), out_specs=(spec, spec), check_vma=False
    )
```

```python
import math

import jax
import jax.numpy as jnp
from jax import lax
from jax.experimental import pallas as pl
from jax.experimental.pallas import tpu as pltpu
from jax.sharding import Mesh, PartitionSpec as P

F32 = jnp.float32
BF16 = jnp.bfloat16
NLON, NLAT, ORDERS, DEGREES = 1440, 704, 384, 384
ROWS, POINTS, CH = 22, 180, 256
RING = ("zlo", "zhi", "y")
CROSS = ("x", "core")
NT = (((1,), (1,)), ((), ()))
TN = (((0,), (0,)), ((), ()))
SMEM = pl.BlockSpec(memory_space=pltpu.SMEM)
PIECE = jax.ShapeDtypeStruct((768, 128), BF16)


def call(body, outs, ins, grid=(1,), scratch=(), us=1, specs=None, out_specs=None, name=None):
    whole = lambda a: pl.BlockSpec(a.shape, lambda *_, n=len(a.shape): (0,) * n)
    specs = specs or [None] * len(ins)
    return pl.pallas_call(
        body,
        out_shape=outs,
        grid=grid,
        in_specs=[whole(a) if s is None else s for a, s in zip(ins, specs)],
        out_specs=out_specs or jax.tree.map(whole, outs),
        scratch_shapes=list(scratch),
        compiler_params=pltpu.CompilerParams(vmem_limit_bytes=56 * 2**20),
        cost_estimate=pl.CostEstimate(
            flops=us * 1_100_000_000, bytes_accessed=us * 1_000_000, transcendentals=0
        ),
        name=name,
    )(*ins)


def partner(position, k):
    dx, dc = divmod(k, 2)
    x, core = position // 2, position % 2
    core = (core + dc) % 2
    return ((x + dx) % 4) * 2 + core, ((x + 4 - dx) % 4) * 2 + core


def pack_kernel(p_ref, x_ref, o_ref, s_ref):
    south = p_ref[0] >= 4
    eye = (
        lax.broadcasted_iota(jnp.int32, (CH, CH), 0) == lax.broadcasted_iota(jnp.int32, (CH, CH), 1)
    ).astype(BF16)
    zeros = jnp.zeros((CH, 76), F32)
    for pair in range(11):
        tail = None
        for parity in range(2):
            j = 2 * pair + parity
            j = jnp.where(south, 21 - j, j)
            head = lax.dot_general(eye, x_ref[j, 0:128, :], NT, preferred_element_type=F32)
            row = (parity * 11 + pair) * 8
            s_ref[:, row : row + 8, :] = head.reshape(32, 8, 128)
            rest = lax.dot_general(eye, x_ref[j, 128:180, :], NT, preferred_element_type=F32)
            rest = jnp.concatenate([rest, zeros], axis=1)
            tail = rest if parity == 0 else tail + pltpu.roll(rest, 64, 1)
        row = 176 + pair * 8
        s_ref[:, row : row + 8, :] = tail.reshape(32, 8, 128)
    o_ref[...] = s_ref[...].astype(BF16)


def pack(position, x):
    return call(
        pack_kernel,
        jax.ShapeDtypeStruct((32, 264, 128), BF16),
        [position, x],
        scratch=[pltpu.VMEM((32, 264, 128), F32)],
        specs=[SMEM, None],
        us=5,
        name="pack",
    )


def waves_kernel(c_ref, s_ref, f_ref, b_ref):
    for d in range(8):
        rows = slice(d * 96, d * 96 + 96)
        order = 8 * (lax.broadcasted_iota(jnp.int32, (96, 128), 0) // 2) + d
        factor = jnp.where(order == 0, 1.0 / NLON, 2.0 / NLON)
        low = lax.broadcasted_iota(jnp.int32, (96, 128), 1) < 64

        def turned(o, lanes):
            angle = (d * o) % 8 * math.pi / 4
            return c_ref[rows, lanes] * math.cos(angle) - s_ref[rows, lanes] * math.sin(angle)

        def put(value, place):
            f_ref[rows, place * 128 : place * 128 + 128] = value.astype(BF16)
            b_ref[rows, place * 128 : place * 128 + 128] = (value * factor).astype(BF16)

        for o in range(8):
            put(turned(o, slice(0, 128)), o)
        for o in range(4):
            tails = [turned(2 * o + i, slice(128, 256)) for i in range(2)]
            put(jnp.where(low, tails[0], tails[1]), 8 + o)


def fourier_tables():
    q = jnp.arange(768, dtype=jnp.int32)
    order, quarter = 8 * (q % 96 // 2) + q // 96, q % 2
    lane = jnp.arange(256, dtype=jnp.int32)
    point = jnp.where(lane < 128, lane, 128 + lane % 64)
    valid = (point < POINTS)[None, :]
    phase = (point[None, :] * order[:, None] + 360 * quarter[:, None]) % NLON
    angle = phase.astype(F32) * (2.0 * math.pi / NLON)
    table = jax.ShapeDtypeStruct((768, 1536), BF16)
    return call(
        waves_kernel,
        (table, table),
        [jnp.where(valid, jnp.cos(angle), 0.0), jnp.where(valid, jnp.sin(angle), 0.0)],
        us=4,
        name="waves",
    )


def fourier_kernel(p_ref, r_ref, f_ref, w_ref, *refs):
    o_refs, (s_ref, k_ref, t_ref) = refs[:8], refs[8:]
    position = p_ref[0]
    south = position >= 4
    s_ref[0 : 32 * 264, :] = r_ref[...].reshape(32 * 264, 128).astype(F32)
    s_ref[32 * 264 :, :] = jnp.zeros((64, 128), F32)
    low = lax.broadcasted_iota(jnp.int32, (16, 128), 1) < 64

    def one(pair, _):
        for b in range(2):
            c = 2 * pair + b
            for zlo in range(4):
                source = jnp.where(south, 3 - zlo, zlo) * (8 * 264) + c
                row = b * 128 + zlo * 32
                tails = []
                for o in range(8):
                    base = source + o * 264
                    for parity in range(2):
                        k_ref[row + parity * 16 : row + parity * 16 + 16, o * 128 : o * 128 + 128] = (
                            s_ref[pl.ds(base + parity * 88, 16, stride=8), :].astype(BF16)
                        )
                    tails.append(s_ref[pl.ds(base + 176, 16, stride=8), :])
                for o in range(4):
                    even, odd = tails[2 * o], tails[2 * o + 1]
                    lanes = slice(1024 + o * 128, 1152 + o * 128)
                    north = jnp.where(low, even, pltpu.roll(odd, 64, 1))
                    k_ref[row : row + 16, lanes] = north.astype(BF16)
                    other = jnp.where(low, pltpu.roll(even, 64, 1), odd)
                    k_ref[row + 16 : row + 32, lanes] = other.astype(BF16)
        spec = lax.dot_general(f_ref[...], k_ref[...], NT, preferred_element_type=F32)
        for b in range(2):
            value = spec[:, b * 128 : b * 128 + 128] * w_ref[0:1, :]
            t_ref[pl.ds(2 * pair + b, 768, stride=8), :] = value
        return 0

    lax.fori_loop(0, 4, one, 0)
    for k in range(8):
        start = pl.multiple_of(partner(position, k)[0] * 768, 768)
        o_refs[k][...] = t_ref[pl.ds(start, 768), :].astype(BF16)


def fourier(position, received, table, weights, us):
    return call(
        fourier_kernel,
        (PIECE,) * 8,
        [position, received, table, weights],
        scratch=[
            pltpu.VMEM((32 * 264 + 64, 128), F32),
            pltpu.VMEM((256, 1536), BF16),
            pltpu.VMEM((6144, 128), F32),
        ],
        specs=[SMEM, None, None, None],
        us=us,
        name="fourier",
    )


def block_orders(i):
    return jnp.where(i < 6, i // 3, jnp.where(i < 10, 2 + (i - 6) // 2, i - 6))


def block_degrees(i):
    return jnp.where(i < 6, i % 3, jnp.where(i < 10, 1 + i % 2, 2))


def table_kernel(m_ref, cos_ref, log_ref, o_ref, s_ref, v_ref):
    i = pl.program_id(0)
    group, part = block_orders(i), block_degrees(i)

    @pl.when(part == group // 2)
    def _():
        v_ref[0] = jnp.zeros((8, 512), F32)
        v_ref[1] = jnp.zeros((8, 512), F32)
        v_ref[2] = log_ref[...]

    order = m_ref[...]
    square = order * order
    cosine = cos_ref[...]
    wide = lambda a: jnp.concatenate([a] * 4, axis=1)

    def steps(n, carried):
        previous, earlier, scale = carried
        size = jnp.exp(scale)
        first = jnp.full((8, 128), part * 128 + n * 8, jnp.int32).astype(F32)

        def ratios(degree):
            above = jnp.maximum(4.0 * degree * degree - 1.0, 0.0)
            below = jnp.maximum(degree * degree - square, 0.0)
            root = lax.rsqrt(jnp.maximum(above * below, 1e-6))
            return above * root, below * root

        _, shrink = ratios(jnp.maximum(first - 1.0, 0.0))
        for u in range(8):
            l = n * 8 + u
            degree = first + float(u)
            growth, inverse_growth = ratios(degree)
            current = wide(growth) * (cosine * previous) - wide(growth * shrink) * earlier
            shrink = inverse_growth
            current = jnp.where(wide(degree == order), 1.0, current)
            value = current * size
            for d in range(4):
                s_ref[d, pl.ds(pl.multiple_of(l * 8, 8), 8), :] = value[:, d * 128 : d * 128 + 128]
            previous, earlier = current, previous
        over = jnp.maximum(jnp.abs(previous), jnp.abs(earlier)) > 1e5
        factor = jnp.where(over, 1e-10, 1.0)
        scale = scale + jnp.where(over, math.log(1e10), 0.0)
        return previous * factor, earlier * factor, scale

    state = lax.fori_loop(0, 16, steps, (v_ref[0], v_ref[1], v_ref[2]))
    for n in range(3):
        v_ref[n] = state[n]
    for s in range(8):
        for d in range(4):
            o_ref[0, s, :, d * 128 : d * 128 + 128] = s_ref[
                d, pl.ds(s, 128, stride=8), :
            ].astype(BF16)


def legendre_table(orders, cosine, logs):
    return call(
        table_kernel,
        jax.ShapeDtypeStruct((12, 8, 128, 512), BF16),
        [orders, cosine, logs],
        grid=(12,),
        scratch=[pltpu.VMEM((4, 1024, 128), F32), pltpu.VMEM((3, 8, 512), F32)],
        specs=[
            pl.BlockSpec((8, 128), lambda i: (block_orders(i), 0)),
            None,
            pl.BlockSpec((8, 512), lambda i: (block_orders(i), 0)),
        ],
        out_specs=pl.BlockSpec((1, 8, 128, 512), lambda i: (i, 0, 0, 0)),
        us=25,
        name="legendre",
    )


def pick(g, *values):
    out = values[-1]
    for n in reversed(range(len(values) - 1)):
        out = jnp.where(g == n, values[n], out)
    return out


TABLE = [
    pl.BlockSpec((1, 8, 128, 512), lambda g, v=v: (pick(g, *v), 0, 0, 0))
    for v in ((0, 3), (1, 4, 6, 8), (2, 5, 7, 9, 10, 11))
]


def by_parts(group, body):
    for first in range(3):

        @pl.when(group // 2 == first)
        def _(first=first):
            body(first)


def signs(position, rows):
    lane = lax.broadcasted_iota(jnp.int32, (rows, 128), 1)
    return jnp.where((lane + position) % 2 == 0, 1.0, -1.0)


def analyse_kernel(p_ref, *refs):
    pieces, t_refs, (o_ref, s_ref, c_ref, q_ref) = refs[:8], refs[8:11], refs[11:]
    group = pl.program_id(0)
    position = p_ref[0]

    @pl.when(group == 0)
    def _():
        for k in range(8):
            s_ref[partner(position, k)[1]] = pieces[k][...]
        c_ref[...] = jnp.zeros_like(c_ref)

    sign = signs(position, 16)

    def body(first):
        for s in range(8):
            row = pl.multiple_of(group * 128 + s * 16, 16)
            north = jnp.concatenate([s_ref[d, pl.ds(row, 16), :] for d in range(4)], axis=1)
            south = jnp.concatenate([s_ref[7 - d, pl.ds(row, 16), :] for d in range(4)], axis=1)
            value = lax.dot_general(
                jnp.concatenate([north, south], axis=0),
                jnp.concatenate([t_refs[b][0, s] for b in range(first, 3)], axis=0),
                NT,
                preferred_element_type=F32,
            )
            for b in range(first, 3):
                lanes = slice((b - first) * 128, (b - first) * 128 + 128)
                c_ref[b, pl.ds(row, 16), :] = value[0:16, lanes] + sign * value[16:32, lanes]

    by_parts(group, body)

    @pl.when(group == 5)
    def _():
        lane = lax.broadcasted_iota(jnp.int32, (96, 128), 1)
        for c in range(8):
            block = jnp.concatenate(
                [c_ref[b, pl.ds(c, 96, stride=8), :] for b in range(3)], axis=1
            )
            block = jnp.concatenate([block, jnp.zeros((32, DEGREES), F32)], axis=0).T
            first = jnp.where(lane < 96, block[288:384], pltpu.roll(block[0:96], 96, 1))
            second = jnp.where(lane < 72, block[192:288], pltpu.roll(block[96:192], 72, 1))
            q_ref[0, pl.ds(c, 96, stride=8), :] = first
            q_ref[1, pl.ds(c, 96, stride=8), :] = second
        o_ref[...] = jnp.concatenate(
            [q_ref[0].reshape(32, 24, 128), q_ref[1].reshape(32, 24, 128)], axis=1
        ).astype(BF16)


def analyse(position, pieces, table):
    return call(
        analyse_kernel,
        jax.ShapeDtypeStruct((32, 48, 128), BF16),
        [position, *pieces, table, table, table],
        grid=(6,),
        scratch=[
            pltpu.VMEM((8, 768, 128), BF16),
            pltpu.VMEM((3, 768, 128), F32),
            pltpu.VMEM((2, 768, 128), F32),
        ],
        specs=[SMEM] + [None] * 8 + TABLE,
        us=10,
        name="analyse",
    )


def pair_rows(ref, p):
    return ref[:, p * 8 : p * 8 + 8, :].astype(F32).reshape(CH, 128).astype(BF16)


def mix_kernel(a_ref, w_ref, o_ref):
    lane = lax.broadcasted_iota(jnp.int32, (CH, 128), 1)
    pieces = []
    for p in range(6):
        half, e = divmod(p, 3)
        rows = pair_rows(a_ref, p)
        high = jnp.dot(w_ref[3 - half, :, e].reshape(CH, CH), rows, preferred_element_type=F32)
        low = jnp.dot(w_ref[half, :, e].reshape(CH, CH), rows, preferred_element_type=F32)
        pieces.append(jnp.where(lane < 96 - 24 * half, high, low).reshape(32, 8, 128))
    o_ref[...] = jnp.concatenate(pieces, axis=1).astype(BF16)


def mix(adjoint, mixing):
    return call(
        mix_kernel,
        jax.ShapeDtypeStruct((32, 48, 128), BF16),
        [adjoint, mixing],
        us=3,
        name="mix",
    )


PARTS = jax.ShapeDtypeStruct((4, 3, 128, CH), F32)


def grad_kernel(p_ref, c_ref, a_ref, near_ref, far_ref, s_ref):
    lane = lax.broadcasted_iota(jnp.int32, (CH, 128), 1)
    for p in range(6):
        half, e = divmod(p, 3)
        left, right = pair_rows(c_ref, p), pair_rows(a_ref, p)
        inside = lane < 96 - 24 * half
        zero = jnp.zeros_like(left)
        high = lax.dot_general(jnp.where(inside, left, zero), right, NT, preferred_element_type=F32)
        low = lax.dot_general(jnp.where(inside, zero, left), right, NT, preferred_element_type=F32)
        for n in range(2):
            s_ref[2 * (3 - half) + n, e] = high[n * 128 : n * 128 + 128]
            s_ref[2 * half + n, e] = low[n * 128 : n * 128 + 128]
    for dx in range(4):
        near_ref[dx] = s_ref[partner(p_ref[0], 2 * dx)[0]]
        far_ref[dx] = s_ref[partner(p_ref[0], 2 * dx + 1)[0]]


def weight_sums(position, coefficients, adjoint):
    return call(
        grad_kernel,
        (PARTS, PARTS),
        [position, coefficients, adjoint],
        scratch=[pltpu.VMEM((8, 3, 128, CH), F32)],
        specs=[SMEM, None, None],
        us=4,
        name="grad",
    )


def add_kernel(a_ref, b_ref, *o_refs):
    for dx in range(4):
        o_refs[dx][...] = a_ref[dx] + b_ref[dx]


def add_cores(near, far):
    piece = jax.ShapeDtypeStruct((3, 128, CH), F32)
    return call(add_kernel, (piece,) * 4, [near, far], us=3, name="add")


def total_kernel(y_ref, *refs):
    pieces, o_refs, s_ref = refs[:4], refs[4:8], refs[8]
    s_ref[...] = (pieces[0][...] + pieces[1][...]) + (pieces[2][...] + pieces[3][...])
    for step in range(4):
        row = pl.multiple_of((y_ref[0] + step) % 4 * 32, 32)
        o_refs[step][...] = s_ref[:, pl.ds(row, 32), :]


def total_sums(y, pieces):
    return call(
        total_kernel,
        (jax.ShapeDtypeStruct((3, 32, CH), F32),) * 4,
        [y, *pieces],
        scratch=[pltpu.VMEM((3, 128, CH), F32)],
        specs=[SMEM] + [None] * 4,
        us=3,
        name="total",
    )


def gather_kernel(p_ref, *refs):
    for k in range(8):
        refs[8][partner(p_ref[0], k)[1]] = refs[k][...]


def gather(position, pieces):
    return call(
        gather_kernel,
        jax.ShapeDtypeStruct((8, 3, 128, CH), BF16),
        [position, *pieces],
        specs=[SMEM] + [None] * 8,
        us=2,
        name="gather",
    )


def synthesise_kernel(p_ref, m_ref, w_ref, *refs):
    t_refs, o_refs, (q_ref, c_ref, b_ref) = refs[:3], refs[3:11], refs[11:]
    group = pl.program_id(0)
    position = p_ref[0]

    @pl.when(group == 0)
    def _():
        mixed = m_ref[...].astype(F32)
        q_ref[0] = mixed[:, 0:24, :].reshape(768, 128)
        q_ref[1] = mixed[:, 24:48, :].reshape(768, 128)
        for c in range(8):
            first = q_ref[0, pl.ds(c, 96, stride=8), :]
            second = q_ref[1, pl.ds(c, 96, stride=8), :]
            block = jnp.concatenate(
                [pltpu.roll(first, 32, 1), pltpu.roll(second, 56, 1), second, first], axis=0
            )
            block = block.T[0:96, :]
            for b in range(3):
                c_ref[b, pl.ds(c, 96, stride=8), :] = block[:, b * 128 : b * 128 + 128]

    sign = signs(position, 16)

    def body(first):
        for s in range(8):
            row = pl.multiple_of(group * 128 + s * 16, 16)
            north = [c_ref[b, pl.ds(row, 16), :] for b in range(first, 3)]
            south = [a * sign for a in north]
            left = jnp.concatenate(
                [jnp.concatenate(north, axis=1), jnp.concatenate(south, axis=1)], axis=0
            ).astype(BF16)
            right = jnp.concatenate([t_refs[b][0, s] for b in range(first, 3)], axis=0)
            value = jnp.dot(left, right, preferred_element_type=F32)
            for d in range(4):
                lanes = slice(d * 128, d * 128 + 128)
                mirror = slice((7 - d) * 128, (7 - d) * 128 + 128)
                b_ref[d, pl.ds(row, 16), :] = (value[0:16, lanes] * w_ref[0:1, lanes]).astype(BF16)
                b_ref[7 - d, pl.ds(row, 16), :] = (
                    value[16:32, lanes] * w_ref[0:1, mirror]
                ).astype(BF16)

    by_parts(group, body)

    @pl.when(group == 5)
    def _():
        for k in range(8):
            o_refs[k][...] = b_ref[partner(position, k)[0]]


def synthesise(position, mixed, table, weights):
    return call(
        synthesise_kernel,
        (PIECE,) * 8,
        [position, mixed, weights, table, table, table],
        grid=(6,),
        scratch=[
            pltpu.VMEM((2, 768, 128), F32),
            pltpu.VMEM((3, 768, 128), F32),
            pltpu.VMEM((8, 768, 128), BF16),
        ],
        specs=[SMEM, None, None] + TABLE,
        us=10,
        name="synthesise",
    )


def inverse_kernel(p_ref, *refs):
    pieces, (f_ref, o_ref, s_ref, t_ref) = refs[:8], refs[8:]
    position = p_ref[0]
    south = position >= 4
    for k in range(8):
        start = pl.multiple_of(partner(position, k)[1] * 768, 768)
        s_ref[pl.ds(start, 768), :] = pieces[k][...].astype(F32)
    low = lax.broadcasted_iota(jnp.int32, (11, 128), 1) < 64

    def one(pair, _):
        left = jnp.concatenate(
            [s_ref[pl.ds(2 * pair + b, 768, stride=8), :].astype(BF16) for b in range(2)], axis=1
        )
        grid = lax.dot_general(left, f_ref[...], TN, preferred_element_type=F32)
        for b in range(2):
            for zlo in range(4):
                place = jnp.where(south, 3 - zlo, zlo) * (8 * 264) + 2 * pair + b
                row = b * 128 + zlo * 32
                even, odd = grid[row : row + 11], grid[row + 16 : row + 27]
                for o in range(8):
                    base = place + o * 264
                    lanes = slice(o * 128, o * 128 + 128)
                    t_ref[pl.ds(base, 11, stride=8), :] = even[:, lanes]
                    t_ref[pl.ds(base + 88, 11, stride=8), :] = odd[:, lanes]
                    lanes = slice(1024 + o // 2 * 128, 1152 + o // 2 * 128)
                    first, last = even[:, lanes], odd[:, lanes]
                    if o % 2 == 0:
                        tail = jnp.where(low, first, pltpu.roll(last, 64, 1))
                    else:
                        tail = jnp.where(low, pltpu.roll(first, 64, 1), last)
                    t_ref[pl.ds(base + 176, 11, stride=8), :] = tail
        return 0

    lax.fori_loop(0, 4, one, 0)
    o_ref[...] = t_ref[...].reshape(32, 264, 128).astype(BF16)


def inverse(position, pieces, table):
    return call(
        inverse_kernel,
        jax.ShapeDtypeStruct((32, 264, 128), BF16),
        [position, *pieces, table],
        scratch=[pltpu.VMEM((6144, 128), F32), pltpu.VMEM((32 * 264, 128), F32)],
        specs=[SMEM] + [None] * 9,
        us=9,
        name="inverse",
    )


def finish_kernel(p_ref, r_ref, g_ref, o_ref, s_ref):
    south = p_ref[0] >= 4
    s_ref[...] = r_ref[...].astype(F32)
    for pair in range(11):
        row = 176 + pair * 8
        tail = s_ref[:, row : row + 8, :].reshape(CH, 128).T
        for parity in range(2):
            j = 2 * pair + parity
            j = jnp.where(south, 21 - j, j)
            row = (parity * 11 + pair) * 8
            head = s_ref[:, row : row + 8, :].reshape(CH, 128).T
            o_ref[j, 0:128, :] = (g_ref[j, 0:128, :].astype(F32) + head).astype(BF16)
            rest = tail[parity * 64 : parity * 64 + 52]
            o_ref[j, 128:180, :] = (g_ref[j, 128:180, :].astype(F32) + rest).astype(BF16)


def finish(position, received, cotangent):
    return call(
        finish_kernel,
        jax.ShapeDtypeStruct((ROWS, POINTS, CH), BF16),
        [position, received, cotangent],
        scratch=[pltpu.VMEM((32, 264, 128), F32)],
        specs=[SMEM, None, None],
        us=4,
        name="finish",
    )


def swap(value):
    return lax.all_to_all(value, RING, split_axis=0, concat_axis=0, tiled=True)


def cross(pieces):
    moved = [pieces[0]]
    for k in range(1, 8):
        pairs = [(p, partner(p, k)[0]) for p in range(8)]
        moved.append(lax.ppermute(pieces[k], CROSS, pairs))
    return moved


def along_x(pieces):
    return [pieces[0]] + [
        lax.ppermute(pieces[dx], "x", [(i, (i + dx) % 4) for i in range(4)]) for dx in range(1, 4)
    ]


def other_core(value):
    return lax.ppermute(value, "core", [(0, 1), (1, 0)])


def turned(pieces):
    moved = []
    for step, piece in enumerate(pieces):
        pairs = [
            (core * 8 + zhi * 4 + y, zhi * 8 + core * 4 + (y + step) % 4)
            for core in range(2)
            for zhi in range(2)
            for y in range(4)
        ]
        moved.append(lax.ppermute(piece, ("core", "zhi", "y"), pairs))
    return moved


def in_order(pieces):
    y = lax.axis_index("y")
    out = jnp.zeros((4, *pieces[0].shape), pieces[0].dtype)
    for step, piece in enumerate(pieces):
        out = lax.dynamic_update_index_in_dim(out, piece, (y + 4 - step) % 4, 0)
    return out


def after(value, *others):
    return lax.optimization_barrier((value, *others))[0]


def slot_rows():
    slot = jnp.arange(512, dtype=jnp.int32)
    device, within = slot // 128, slot % 128
    zlo, parity, pair = within // 32, within % 32 // 16, within % 16
    row = (device // 2) * 176 + zlo * 44 + (device % 2) * 22 + 2 * pair + parity
    mirrored = (NLAT - 1 - row).reshape(4, 128)[::-1].reshape(512)
    valid = pair < 11
    return jnp.concatenate([row, mirrored]), jnp.concatenate([valid, valid])


def local(grid_input, cotangent, mixing):
    position = lax.axis_index("x") * 2 + lax.axis_index("core")
    y = lax.axis_index("y")
    where = jnp.full((1,), position, jnp.int32)
    packed_g = pack(where, cotangent)
    sent_g = swap(packed_g)
    packed_x = pack(where, after(grid_input, packed_g))
    mixing = after(mixing, packed_g)
    weights = in_order(
        turned([lax.dynamic_slice_in_dim(mixing, (y + step) % 4 * 3, 3, 0) for step in range(4)])
    )
    weights = jnp.transpose(weights, (1, 0, 2, 3)).reshape(3, 128, CH)
    row, valid = slot_rows()
    colatitude = (row.astype(F32) + 0.5) * (math.pi / NLAT)
    sine = jnp.sin(colatitude)
    quadrature = jnp.where(valid, math.pi / NLAT * sine, 0.0)
    cosine = jnp.where(valid, jnp.cos(colatitude), 0.0)[0:512]
    orders = 8 * jnp.arange(48, dtype=jnp.int32) + position
    order_value = orders.astype(F32)[:, None]
    counter = jnp.arange(1, ORDERS + 1, dtype=F32)[None, :]
    log_terms = jnp.where(counter <= order_value, jnp.log1p(0.5 / counter), 0.0)
    logs = (
        0.5 * math.log(0.5)
        + 0.5 * jnp.sum(log_terms, axis=1, keepdims=True)
        + order_value * jnp.log(sine[0:512])[None, :]
    )
    logs = jnp.where(valid[None, 0:512], logs, -1e30)
    table = legendre_table(
        after(jnp.broadcast_to(order_value, (48, 128)), packed_x),
        jnp.broadcast_to(cosine[None, :], (8, 512)),
        logs,
    )
    forward, backward = fourier_tables()
    own = lax.dynamic_slice_in_dim(quadrature, position * 128, 128)
    sent_g = after(sent_g, packed_x, forward, backward, table, weights)
    sent_x = swap(after(packed_x, sent_g))
    pieces_g = fourier(where, sent_g, backward, jnp.ones((8, 128), F32), 9)
    packed_adjoint = analyse(where, cross(pieces_g), table)
    adjoint = swap(after(packed_adjoint, sent_x))
    weights = along_x([after(weights, packed_adjoint, sent_x)] * 4)
    weights = [w for near in weights for w in (near, other_core(near))]
    weights = gather(where, weights).reshape(4, 2, 3, 128, CH)
    pieces_x = fourier(where, sent_x, forward, jnp.broadcast_to(own[None, :], (8, 128)), 9)
    mixed = swap(mix(after(adjoint, pieces_x[0]), weights))
    coefficients = analyse(where, cross(pieces_x), table)
    mixed = after(mixed, coefficients)
    back = synthesise(where, mixed, table, jnp.broadcast_to(quadrature[None, :], (8, 1024)))
    coefficients = swap(after(coefficients, back[0]))
    packed_back = inverse(where, cross(back), forward)
    grid_back = swap(packed_back)
    near, far = weight_sums(where, after(coefficients, packed_back), adjoint)
    total = along_x(add_cores(near, other_core(far)))
    total = turned(total_sums(jnp.full((1,), y, jnp.int32), total))
    input_grad = finish(where, grid_back, cotangent)
    total[0] = after(total[0], input_grad)
    return input_grad, in_order(total).reshape(12, 32, CH)


def solution(mesh):
    fine = Mesh(mesh.devices.reshape(4, 4, 2, 2, 4), ("x", "zlo", "core", "zhi", "y"))
    spec = P(("x", "zlo", "core"), ("zhi", "y"), None)
    return jax.shard_map(
        local, mesh=fine, in_specs=(spec, spec, spec), out_specs=(spec, spec), check_vma=False
    )
```
